256 devices in a mesh: dp: 4 (over y), pipe: 4 (over x), expert: 16 (over z, core).
Axes of the slice: x: 4, y: 4, z: 8, core: 2. Of those that a mesh axis runs over, the one named last changes fastest.
Arguments:
- embedded: bfloat16 [3, 512, 2048], P(None, ('dp', 'expert')), may hold values from -6 to 6
- out_grad: bfloat16 [3, 512, 2048], P(None, ('dp', 'expert')), may hold values from -6 to 6
- norm_gain: float32 [4, 2048], P('pipe'), may hold values from 0.1 to 1.9
- router_weight: bfloat16 [4, 2048, 16], P('pipe'), may hold values from -0.5 to 0.5
- gate_weight: bfloat16 [4, 16, 2048, 768], P('pipe', 'expert'), may hold values from -0.125 to 0.125
- up_weight: bfloat16 [4, 16, 2048, 768], P('pipe', 'expert'), may hold values from -0.125 to 0.125
- down_weight: bfloat16 [4, 16, 768, 2048], P('pipe', 'expert'), may hold values from -0.21875 to 0.21875
- routing: int32 [4, 3, 512, 8], P('pipe', None, ('dp', 'expert')), may hold values from 0 to 15, all different within a row; in each aligned block of 8 rows (0 to 7, 8 to 15, ..., all dimensions but the last counted through in order) at most 8 rows name the same one
Outputs:
- activations: bfloat16 [4, 3, 512, 2048], P('pipe', None, ('dp', 'expert'))
- input_grads: bfloat16 [4, 3, 512, 2048], P('pipe', None, ('dp', 'expert'))
- gate_grad: bfloat16 [4, 16, 2048, 768], P('pipe', 'expert', 'dp')
- up_grad: bfloat16 [4, 16, 2048, 768], P('pipe', 'expert', 'dp')
- down_grad: bfloat16 [4, 16, 768, 2048], P('pipe', 'expert', None, 'dp')
- router_grad: float32 [4, 2048, 16], P('pipe', ('dp', 'expert'))
- gain_grad: float32 [4, 2048], P('pipe', ('dp', 'expert'))
The draws below stay inside these ranges and needn't reach their ends.
Inputs may be any that keep to these rules, and one draw needn't show every extreme that they name: `routing`: each row names 8 different experts. In each aligned block of 8 rows (one device's tokens of one micro-batch of one layer) no expert is named by more than 8 rows; in some blocks one expert is named by exactly 8.
All inputs are finite; a program needn't handle non-finite values.
Results may differ from the reference program's by a relative error of at most 0.034.
Values may be sent and summed in bfloat16 or wider, within the bound.
A program may use at most 128 MiB of HBM per device.

```python
import math
import jax
import jax.numpy as jnp
import numpy as np
from jax import lax

D = 2048
F = 768
MB_TOK = 8
MICRO = 3
EXPERTS = 16
TOP = 8
CAP = 8
LAYERS = 4
TOKENS = 512
N_DP = 4
N_EXPERT = 16


def block_scale(rng, shape, pieces, smallest, largest):
    loudness = 1.0
    for dim, shards_of in pieces:
        steps = jax.random.uniform(jax.random.fold_in(jax.random.fold_in(rng, 6), dim), (shards_of,), jnp.float32, smallest / len(pieces), largest / len(pieces))
        loudness = loudness * jnp.repeat(jnp.exp(steps), shape[dim] // shards_of).reshape((-1,) + (1,) * (len(shape) - 1 - dim))
    return loudness


def shared_out(key, own, number, rows, amount, top, reach, lean):
    sequence = jax.random.permutation(key, amount)
    packed, usual = load_shares(amount, rows * top, reach, lean, True), load_shares(amount, rows * top, reach, lean, False)
    places = jnp.arange(amount)

    def named(sizes, turn):
        used = int((sizes > 0).sum())
        fixed = max(1, used // 4)
        moved = fixed + (places - fixed + turn * (used - fixed)) % max(1, amount - fixed)
        return jnp.zeros((amount,), jnp.int32).at[sequence[jnp.where(places < fixed, places, moved)]].set(jnp.asarray(sizes, jnp.int32))

    sizes = jnp.where(number % 4 == 0, named(packed, number // 4), named(usual, number - number // 4 - 1))
    mixed = jax.random.permutation(jax.random.fold_in(own, 3), amount)
    donor, receiver = mixed[0:amount // 2 * 2:2], mixed[1:amount // 2 * 2:2]
    slack = jnp.minimum(sizes[donor] - 1, reach - sizes[receiver]) // 2
    slack = jnp.where((donor == sequence[0]) | (receiver == sequence[0]) | (sizes[receiver] == 0), 0, jnp.maximum(slack, 0))
    moved = jax.random.randint(jax.random.fold_in(own, 4), (amount // 2,), 0, 1 << 20) % (slack + 1)
    sizes = sizes.at[donor].add(-moved).at[receiver].add(moved)
    labels = jnp.searchsorted(jnp.cumsum(sizes), jnp.arange(rows * top), side="right").astype(jnp.int32)
    grid = labels.reshape(top, rows).T
    grid = grid[jax.random.permutation(jax.random.fold_in(own, 1), rows)]
    turn = jax.random.randint(jax.random.fold_in(own, 2), (rows, 1), 0, top)
    return jnp.take_along_axis(grid, (jnp.arange(top)[None, :] + turn) % top, axis=1)


def load_shares(amount, total, reach, skew, full):
    portions = [(1 << 20) // math.isqrt(rank ** skew) + 1 for rank in range(1, amount + 1)]
    largest = reach if full else min(reach, max(-(-total // amount), total * portions[0] // sum(portions)))
    least = 1 if total - largest >= amount - 1 else 0
    given, spare = [largest] + [least] * (amount - 1), total - largest - least * (amount - 1)
    while spare > 0:
        candidates = [i for i in range(1, amount) if given[i] < largest] or [i for i in range(1, amount) if given[i] < reach]
        pool, remaining = sum([portions[i] for i in candidates]), spare
        for i in candidates:
            addition = min(reach - given[i], max(1, remaining * portions[i] // pool), spare)
            given[i] = given[i] + addition
            spare = spare - addition
    return np.array(given)


def noise(stream_key, extent, scale, limit, split=(), kind=jnp.bfloat16):
    drawn = scale * jax.random.normal(stream_key, extent, jnp.float32)
    if split:
        drawn = drawn * block_scale(stream_key, extent, split, -0.22, 0.18)
    return jnp.clip(drawn, -limit, limit).astype(kind)


def setup_inputs(seed: int = 0) -> dict:
    key_of = jax.random.split(jax.random.key(seed), 9)
    embedded = noise(key_of[0], (MICRO, TOKENS, D), 1.0, 6.0, ((1, 64),))
    out_grad = noise(key_of[1], (MICRO, TOKENS, D), 1.0, 6.0, ((1, 64),))
    norm_gain = jnp.clip(1.0 + 0.18 * jax.random.normal(key_of[2], (LAYERS, D), jnp.float32), 0.1, 1.9)
    router_weight = noise(key_of[3], (LAYERS, D, EXPERTS), (D // 16) ** -0.5, 0.5, ((0, 4),))
    gate_weight = noise(key_of[4], (LAYERS, EXPERTS, D, F), D ** -0.5, 0.125, ((0, 4), (1, 16)))
    up_weight = noise(key_of[5], (LAYERS, EXPERTS, D, F), D ** -0.5, 0.125, ((0, 4), (1, 16)))
    down_weight = noise(key_of[6], (LAYERS, EXPERTS, F, D), F ** -0.5, 0.21875, ((0, 4), (1, 16)))
    routing_keys = jax.random.split(jax.random.fold_in(key_of[7], 1), LAYERS * MICRO * TOKENS // MB_TOK)
    routing_turns = jax.random.permutation(jax.random.fold_in(key_of[7], 3), LAYERS * MICRO * TOKENS // MB_TOK)
    routing = jax.vmap(lambda own, number: shared_out(jax.random.fold_in(key_of[7], 2), own, number, MB_TOK, EXPERTS, TOP, CAP, 2))(routing_keys, routing_turns).reshape((LAYERS, MICRO, TOKENS, TOP))
    return {"embedded": embedded, "out_grad": out_grad, "norm_gain": norm_gain, "router_weight": router_weight, "gate_weight": gate_weight, "up_weight": up_weight, "down_weight": down_weight, "routing": routing}


BEST = lax.Precision.HIGHEST
EPSILON = 1e-06

def normalize(layer_input, gain_row):
    wide_input = layer_input.astype(jnp.float32)
    inv_rms = lax.rsqrt(lax.optimization_barrier(jnp.mean(wide_input * wide_input, axis=-1, keepdims=True)) + EPSILON)
    return ((wide_input * inv_rms * gain_row).astype(jnp.bfloat16), wide_input, inv_rms)

def slot_table(ids, expert_count):
    token_count, top_count = ids.shape
    flat_ids = ids.reshape(token_count * top_count)
    member = (flat_ids[:, None] == jnp.arange(expert_count, dtype=jnp.int32)[None, :]).astype(jnp.int32)
    earlier = jnp.cumsum(member, axis=0) - member
    slot_place = flat_ids * CAP + lax.optimization_barrier(jnp.sum(earlier * member, axis=1))
    onehot = (slot_place[:, None] == jnp.arange(expert_count * CAP, dtype=jnp.int32)[None, :]).astype(jnp.float32)
    return onehot.reshape(token_count, top_count, expert_count * CAP)

def route(normed, router_map, ids):
    logits = jnp.einsum('btd,de->bte', normed.astype(jnp.float32), router_map.astype(jnp.float32), precision=BEST)
    probs = jax.nn.sigmoid(logits)
    pick_table = (ids[..., None] == jnp.arange(EXPERTS, dtype=jnp.int32)).astype(jnp.float32)
    chosen = lax.optimization_barrier(jnp.sum(pick_table * probs[..., None, :], axis=-1))
    prob_total = lax.optimization_barrier(jnp.sum(chosen, axis=-1, keepdims=True))
    return (chosen / prob_total, chosen, prob_total, pick_table)

def to_expert(blocked):
    count = blocked.shape[0]
    return blocked.reshape(count, EXPERTS, CAP, D).transpose(1, 0, 2, 3).reshape(EXPERTS, count * CAP, D)

def from_expert(rowwise):
    count = rowwise.shape[1] // CAP
    return rowwise.reshape(EXPERTS, count, CAP, D).transpose(1, 0, 2, 3).reshape(count, EXPERTS * CAP, D)

def layer_forward(layer_input, ids, gain_row, router_map, gate_map, up_map, down_map):
    normed, wide_input, inv_rms = normalize(layer_input, gain_row)
    weights, chosen, prob_total, pick_table = route(normed, router_map, ids)
    onehot = jax.vmap(slot_table, in_axes=(0, None))(ids, EXPERTS)
    spread = lax.optimization_barrier(jnp.sum(onehot, axis=2))
    combine = lax.optimization_barrier(jnp.sum(onehot * weights[..., None], axis=2))
    outgoing = jnp.einsum('btj,btd->bjd', spread, normed.astype(jnp.float32), precision=BEST).astype(jnp.bfloat16)
    row_block = to_expert(outgoing)
    wide_rows = row_block.astype(jnp.float32)
    gate_pre = jnp.einsum('erd,edf->erf', wide_rows, gate_map.astype(jnp.float32), precision=BEST)
    up_pre = jnp.einsum('erd,edf->erf', wide_rows, up_map.astype(jnp.float32), precision=BEST)
    hidden = (jax.nn.silu(gate_pre) * up_pre).astype(jnp.bfloat16)
    expert_out = jnp.einsum('erf,efd->erd', hidden.astype(jnp.float32), down_map.astype(jnp.float32), precision=BEST).astype(jnp.bfloat16)
    returned = from_expert(expert_out)
    mixed = jnp.einsum('btj,bjd->btd', combine, returned.astype(jnp.float32), precision=BEST)
    layer_output = (wide_input + mixed).astype(jnp.bfloat16)
    saved = (normed, wide_input, inv_rms, weights, chosen, prob_total, pick_table, onehot, spread, combine, row_block, gate_pre, up_pre, hidden, returned)
    return (layer_output, saved)

def layer_backward(upstream, saved, gain_row, router_map, gate_map, up_map, down_map):
    normed, wide_input, inv_rms, weights, chosen, prob_total, pick_table, onehot, spread, combine, row_block, gate_pre, up_pre, hidden, returned = saved
    grad_wide = upstream.astype(jnp.float32)
    sent_grad = jnp.einsum('btj,btd->bjd', combine, grad_wide, precision=BEST).astype(jnp.bfloat16)
    rows_grad = to_expert(sent_grad)
    slot_score = jnp.einsum('btd,bjd->btj', grad_wide, returned.astype(jnp.float32), precision=BEST)
    dweight = lax.optimization_barrier(jnp.sum(onehot * slot_score[..., None, :], axis=-1))
    dchosen = (dweight - lax.optimization_barrier(jnp.sum(dweight * weights, axis=-1, keepdims=True))) / prob_total
    dselect = dchosen * chosen * (1.0 - chosen)
    dlogits = lax.optimization_barrier(jnp.sum(pick_table * dselect[..., None], axis=-2))
    wide_grad_rows = rows_grad.astype(jnp.float32)
    dhidden = jnp.einsum('erd,efd->erf', wide_grad_rows, down_map.astype(jnp.float32), precision=BEST)
    sigma_gate = jax.nn.sigmoid(gate_pre)
    activated = gate_pre * sigma_gate
    dgate = (dhidden * up_pre * sigma_gate * (1.0 + gate_pre * (1.0 - sigma_gate))).astype(jnp.bfloat16)
    dup = (dhidden * activated).astype(jnp.bfloat16)
    drows = (jnp.einsum('erf,edf->erd', dgate.astype(jnp.float32), gate_map.astype(jnp.float32), precision=BEST) + jnp.einsum('erf,edf->erd', dup.astype(jnp.float32), up_map.astype(jnp.float32), precision=BEST)).astype(jnp.bfloat16)
    wide_rows = row_block.astype(jnp.float32)
    gate_term = jnp.einsum('erd,erf->edf', wide_rows, dgate.astype(jnp.float32), precision=BEST)
    up_term = jnp.einsum('erd,erf->edf', wide_rows, dup.astype(jnp.float32), precision=BEST)
    down_term = jnp.einsum('erd,erf->edf', wide_grad_rows, hidden.astype(jnp.float32), precision=BEST)
    back_grad = from_expert(drows)
    dnormed = jnp.einsum('btj,bjd->btd', spread, back_grad.astype(jnp.float32), precision=BEST) + jnp.einsum('bte,de->btd', dlogits, router_map.astype(jnp.float32), precision=BEST)
    router_term = jnp.einsum('btd,bte->de', normed.astype(jnp.float32), dlogits, precision=BEST)
    scaled = dnormed * gain_row
    dinput = inv_rms * (scaled - wide_input * (inv_rms * inv_rms) * lax.optimization_barrier(jnp.mean(scaled * wide_input, axis=-1, keepdims=True)))
    gain_term = lax.optimization_barrier(jnp.sum(dnormed * wide_input * inv_rms, axis=(0, 1)))
    layer_grad = (grad_wide + dinput).astype(jnp.bfloat16)
    return (layer_grad, gate_term, up_term, down_term, router_term, gain_term)

def reference(embedded, out_grad, norm_gain, router_weight, gate_weight, up_weight, down_weight, routing):
    block_count = N_DP * N_EXPERT
    layer_outputs = []
    layer_grads = []
    gate_sums = []
    up_sums = []
    down_sums = []
    router_sums = []
    gain_sums = []
    for layer in range(LAYERS):
        layer_outputs.append([None] * MICRO)
        layer_grads.append([None] * MICRO)
        gate_sums.append(jnp.zeros((EXPERTS, D, F), jnp.float32))
        up_sums.append(jnp.zeros((EXPERTS, D, F), jnp.float32))
        down_sums.append(jnp.zeros((EXPERTS, D, F), jnp.float32))
        router_sums.append(jnp.zeros((D, EXPERTS), jnp.float32))
        gain_sums.append(jnp.zeros((D,), jnp.float32))
    for micro_index in range(MICRO):
        current = embedded[micro_index].reshape(block_count, MB_TOK, D)
        saved_list = []
        for layer in range(LAYERS):
            ids = routing[layer, micro_index].reshape(block_count, MB_TOK, TOP)
            current, saved = layer_forward(current, ids, norm_gain[layer], router_weight[layer], gate_weight[layer], up_weight[layer], down_weight[layer])
            saved_list.append(saved)
            layer_outputs[layer][micro_index] = current.reshape(TOKENS, D)
        upstream = out_grad[micro_index].reshape(block_count, MB_TOK, D)
        for layer in range(LAYERS - 1, -1, -1):
            upstream, gate_term, up_term, down_term, router_term, gain_term = layer_backward(upstream, saved_list[layer], norm_gain[layer], router_weight[layer], gate_weight[layer], up_weight[layer], down_weight[layer])
            layer_grads[layer][micro_index] = upstream.reshape(TOKENS, D)
            gate_sums[layer] = gate_sums[layer] + gate_term
            up_sums[layer] = up_sums[layer] + up_term
            down_sums[layer] = down_sums[layer] + down_term
            router_sums[layer] = router_sums[layer] + router_term
            gain_sums[layer] = gain_sums[layer] + gain_term
    activations = jnp.stack([jnp.stack(row) for row in layer_outputs])
    input_grads = jnp.stack([jnp.stack(row) for row in layer_grads])
    gate_grad = jnp.stack(gate_sums).astype(jnp.bfloat16)
    up_grad = jnp.stack(up_sums).astype(jnp.bfloat16)
    down_grad = jnp.stack(down_sums).transpose(0, 1, 3, 2).astype(jnp.bfloat16)
    router_grad = jnp.stack(router_sums)
    gain_grad = jnp.stack(gain_sums)
    return (activations, input_grads, gate_grad, up_grad, down_grad, router_grad, gain_grad)
```

```python
import functools

import jax
import jax.numpy as jnp
from jax import lax
from jax.experimental import pallas as pl
from jax.experimental.pallas import tpu as pltpu
from jax.sharding import PartitionSpec as P

EPSILON = 1e-06
MESH = pl.DeviceIdType.MESH
BF = jnp.bfloat16
F32 = jnp.float32
NN = (((1,), (0,)), ((), ()))
NT = (((1,), (1,)), ((), ()))
TN = (((0,), (0,)), ((), ()))


def dot(a, b, dims):
    return lax.dot_general(a, b, dims, preferred_element_type=F32)


def col(value):
    return jnp.sum(value, axis=-1, keepdims=True)


def kernel(
    sizes,
    emb_ref, og_ref, ids_ref, gain_ref, rw_ref, gate_hbm, up_hbm, down_hbm,
    act_ref, igr_ref, gg_ref, ug_ref, dg_ref, rg_ref,
    wg, wu, wd, ebs, ebr, src0, pmall, xall, nrm, gpre, upre, hidb, invs, wst, lgs,
    ps_f, pr_f, ps_b, pr_b, qo_f, qo_b, qf, qb, rf, rb, actb,
    nsl, gsl, hid, dga, dup, racc, rgs, ybuf, ysum, zbuf,
    w_sem, e_s, e_r, m_s, m_r, ag0_s, ag_s, ag_r, fw_s, fw_r, pr_s, pr_rs, rs_s, rs_r, ac_s, ac_r,
    y_s, y_r, r1_s, r1_r, r2_s, r2_r,
):
    NM, D, F, NE, ND, NP = sizes
    NZ, H, R, DS = NE // 2, D // 2, NE * 8, D // ND
    HX = H + 128
    me_y = lax.axis_index("dp")
    me_l = lax.axis_index("pipe")
    me_e = lax.axis_index("expert")
    z = me_e // 2
    c = me_e % 2
    oc = 1 - c
    partner = {"expert": me_e + 1 - 2 * c}
    own_rows = pl.ds(pl.multiple_of(z * 16, 16), 16)
    own_half = pl.ds(pl.multiple_of(c * H, H), H)
    other_half = pl.ds(pl.multiple_of(oc * H, H), H)
    last = (me_l + 1) // NP

    def send(src, dst, ss, rs, dev):
        pltpu.make_async_remote_copy(
            src_ref=src, dst_ref=dst, send_sem=ss, recv_sem=rs, device_id=dev, device_id_type=MESH
        ).start()

    def copy(src, dst, sem):
        pltpu.make_async_copy(src, dst, sem).start()

    def wait(ref, sem):
        pltpu.make_async_copy(ref, ref, sem).wait()

    copy(gate_hbm, wg, w_sem.at[0])
    copy(up_hbm, wu, w_sem.at[1])
    copy(down_hbm, wd, w_sem.at[2])

    barrier = pltpu.get_barrier_semaphore()

    def hello(dev):
        pl.semaphore_signal(barrier, inc=1, device_id=dev, device_id_type=MESH)

    hello(partner)
    for k in range(1, NZ):
        for cc in range(2):
            hello({"expert": 2 * ((z + k) % NZ) + cc})
    for j in range(1, ND):
        hello({"dp": (me_y + j) % ND})
    for step in (1, NP - 1):
        for k in range(NZ):
            hello({"pipe": (me_l + step) % NP, "expert": 2 * ((z + k) % NZ) + c})

    mine0 = (c == 0).astype(F32)
    for kind, ref in enumerate((emb_ref, og_ref)):
        for m in range(NM):
            v = ref[m].astype(F32)
            blk = jnp.concatenate([v * mine0, v * (1.0 - mine0)], axis=0).astype(BF)
            ebs[kind, 0, m] = blk[:, :H]
            ebs[kind, 1, m] = blk[:, H:]
    lanes8 = lax.broadcasted_iota(jnp.int32, (8, 128), 1)
    for m in range(NM):
        ids = ids_ref[m]
        table = jnp.zeros((8, 128), F32)
        for k in range(ids.shape[1]):
            table = table + (ids[:, k:k + 1] == lanes8).astype(F32)
        pmall[me_e, m] = table
    racc[...] = jnp.zeros(racc.shape, F32)

    pl.semaphore_wait(barrier, 1 + 2 * (NZ - 1) + (ND - 1) + 2 * NZ)

    for kind in range(2):
        send(ebs.at[kind, oc], ebr.at[kind], e_s.at[kind], e_r.at[kind], partner)
    send(pmall.at[me_e], pmall.at[me_e], m_s, m_r, partner)
    for k in range(1, NZ):
        for cc in range(2):
            send(
                pmall.at[me_e], pmall.at[me_e], m_s, m_r, {"expert": 2 * ((z + k) % NZ) + cc}
            )

    def gather_here(kind, m):
        src = src0.at[kind, m]
        dst = xall.at[kind, m, c, own_rows]
        for k in range(1, NZ):
            send(src, dst, ag0_s.at[kind, m], ag_r.at[kind, m], {"expert": 2 * ((z + k) % NZ) + c})
        copy(src, dst, ag_r.at[kind, m])

    def gather_there(kind, m, section):
        for k in range(NZ):
            send(
                actb.at[kind, c, m], xall.at[kind, m, c, own_rows],
                ag_s.at[kind, m], ag_r.at[kind, m],
                {"pipe": section, "expert": 2 * ((z + k) % NZ) + c},
            )

    for kind in range(2):
        wait(ebr.at[kind], e_r.at[kind])
        for m in range(NM):
            src0[kind, m] = (
                ebs[kind, c, m].astype(F32) + ebr[kind, m].astype(F32)
            ).astype(BF)
        if kind == 0:
            @pl.when(me_l == 0)
            def _():
                gather_here(0, 0)
        else:
            @pl.when(last == 1)
            def _():
                for m in range(NM):
                    gather_here(1, m)

    wait(pmall.at[pl.ds(0, NE - 1)], m_r)
    wait(wg, w_sem.at[0])
    wait(wu, w_sem.at[1])
    wait(wd, w_sem.at[2])

    def arrive(kind, m):
        wait(xall.at[kind, m, c], ag_r.at[kind, m])
        send(
            xall.at[kind, m, c], xall.at[kind, m, c], fw_s.at[kind, m], fw_r.at[kind, m], partner
        )
        if kind == 0:
            @pl.when((me_l == 0) & (m < NM - 1))
            def _():
                gather_here(0, m + 1)
        wait(xall.at[kind, m, oc], fw_r.at[kind, m])

    lane_e = lax.broadcasted_iota(jnp.int32, (R, NE), 1)
    lane_x = lax.broadcasted_iota(jnp.int32, (R, 128), 1)

    def forward_compute(m):
        x0 = xall[0, m, 0].astype(F32)
        x1 = xall[0, m, 1].astype(F32)
        inv = lax.rsqrt((col(x0 * x0) + col(x1 * x1)) * (1.0 / D) + EPSILON)
        n0 = (x0 * inv * gain_ref[0:1, :H]).astype(BF)
        n1 = (x1 * inv * gain_ref[0:1, H:]).astype(BF)
        nrm[m, 0] = n0
        nrm[m, 1] = n1
        logits = dot(n0, rw_ref[:H, :], NN) + dot(n1, rw_ref[H:, :], NN)
        named = pmall[:, m].reshape(R, 128)[:, :NE]
        chosen = named * jax.nn.sigmoid(logits)
        w = col(jnp.where(lane_e == me_e, chosen, 0.0)) / col(chosen)
        invs[m] = jnp.broadcast_to(inv, (R, 128))
        wst[m] = jnp.broadcast_to(w, (R, 128))
        lgs[m] = logits
        a = dot(n0, wg[:H, :], NN) + dot(n1, wg[H:, :], NN)
        b = dot(n0, wu[:H, :], NN) + dot(n1, wu[H:, :], NN)
        gpre[m] = a
        upre[m] = b
        h = (a * jax.nn.sigmoid(a) * b).astype(BF)
        hidb[m] = h
        hid[me_y, m] = (h.astype(F32) * w).astype(BF)
        ps_f[m] = (dot(h, wd[:, other_half], NN) * w).astype(BF)
        send(ps_f.at[m], pr_f.at[m], pr_s.at[0, m], pr_rs.at[0, m], partner)
        qo_f[...] = dot(h, wd[:, own_half], NN) * w

    def scatter(kind, m, q, r):
        for k in range(1, NZ):
            zz = (z + k) % NZ
            send(
                q.at[m, pl.ds(pl.multiple_of(zz * 16, 16), 16)], r.at[m, z],
                rs_s.at[kind, m], rs_r.at[kind, m], {"expert": 2 * zz + c},
            )
        copy(q.at[m, own_rows], r.at[m, z], rs_r.at[kind, m])

    def half_slice(ref, yy):
        start = yy * DS
        return ref.at[start // H, :, pl.ds(pl.multiple_of(start % H, 128), DS)]

    def to_replicas(m, whole, halves, slices, base):
        for j in range(1, ND):
            yy = (me_y + j) % ND
            for i, ref in enumerate(whole):
                send(
                    ref.at[me_y, m], ref.at[me_y, m], y_s.at[base + i, m], y_r.at[base + i, m],
                    {"dp": yy},
                )
            i = base + len(whole)
            send(half_slice(halves, yy), slices.at[me_y, m], y_s.at[i, m], y_r.at[i, m], {"dp": yy})
        i = base + len(whole)
        copy(half_slice(halves, me_y), slices.at[me_y, m], y_r.at[i, m])

    def forward_scatter(m):
        wait(pr_f.at[m], pr_rs.at[0, m])
        qf[m] = (qo_f[...] + pr_f[m].astype(F32)).astype(BF)
        scatter(0, m, qf, rf)
        to_replicas(m, (hid,), nrm.at[m], nsl, 0)

    def forward_result(m):
        wait(rf.at[m], rs_r.at[0, m])
        total = xall[0, m, c, own_rows].astype(F32)
        for k in range(NZ):
            total = total + rf[m, k].astype(F32)
        actb[0, c, m] = total.astype(BF)

        @pl.when(last == 0)
        def _():
            gather_there(0, m, me_l + 1)

        send(actb.at[0, c, m], actb.at[0, c, m], ac_s.at[0, m], ac_r.at[0, m], partner)

    def backward_compute(m):
        dh = dot(xall[1, m, 0], wd[:, :H], NT) + dot(xall[1, m, 1], wd[:, H:], NT)
        w = wst[m][:, :1]
        a = gpre[m]
        b = upre[m]
        dw = col(dh * hidb[m].astype(F32))
        dhw = dh * w
        s = jax.nn.sigmoid(a)
        dgate = (dhw * b * s * (1.0 + a * (1.0 - s))).astype(BF)
        dupv = (dhw * (a * s)).astype(BF)
        dga[me_y, m] = dgate
        dup[me_y, m] = dupv
        sv = col(dgate.astype(F32) * a + dupv.astype(F32) * b)
        dw_hi = dw.astype(BF).astype(F32)
        sv_hi = sv.astype(BF).astype(F32)
        ext = jnp.where(lane_x == me_e, dw_hi, 0.0)
        ext = jnp.where(lane_x == NE + me_e, dw - dw_hi, ext)
        ext = jnp.where(lane_x == 2 * NE + me_e, sv_hi, ext)
        ext = jnp.where(lane_x == 3 * NE + me_e, sv - sv_hi, ext)
        ps_b[m, :, :H] = (
            dot(dgate, wg[other_half, :], NT) + dot(dupv, wu[other_half, :], NT)
        ).astype(BF)
        ps_b[m, :, H:] = ext.astype(BF)
        send(ps_b.at[m], pr_b.at[m], pr_s.at[1, m], pr_rs.at[1, m], partner)
        qo_b[:, :H] = dot(dgate, wg[own_half, :], NT) + dot(dupv, wu[own_half, :], NT)
        qo_b[:, H:] = ext

    def backward_scatter(m):
        wait(pr_b.at[m], pr_rs.at[1, m])
        qb[m] = (qo_b[...] + pr_b[m].astype(F32)).astype(BF)
        scatter(1, m, qb, rb)
        to_replicas(m, (dga, dup), xall.at[1, m], gsl, 2)

    def backward_result(m):
        wait(rb.at[m], rs_r.at[1, m])
        total = rb[m, 0].astype(F32)
        for k in range(1, NZ):
            total = total + rb[m, k].astype(F32)
        ext = total[:, H:]
        dw = ext[:, :NE] + ext[:, NE:2 * NE]
        sv = col(ext[:, 2 * NE:3 * NE] + ext[:, 3 * NE:4 * NE])
        logits = lgs[m, own_rows]
        named = pmall[pl.ds(2 * z, 2), m].reshape(16, 128)[:, :NE]
        chosen = named * jax.nn.sigmoid(logits)
        prob_total = col(chosen)
        weights = chosen / prob_total
        dchosen = (dw - col(dw * weights)) / prob_total
        dlogits = dchosen * chosen * (1.0 - chosen)
        dl_hi = dlogits.astype(BF)
        dl_lo = (dlogits - dl_hi.astype(F32)).astype(BF)
        router_half = rw_ref[own_half, :]
        dnormed = total[:, :H] + dot(dl_hi, router_half, NT) + dot(dl_lo, router_half, NT)
        inv = invs[m, own_rows][:, :1]
        gain_half = gain_ref[0:1, own_half]
        x = xall[0, m, c, own_rows].astype(F32)
        g = xall[1, m, c, own_rows].astype(F32)
        normed = nrm[m, c, own_rows]
        along = (sv + col(dlogits * logits)) * (1.0 / D)
        dinput = inv * (dnormed * gain_half - x * (inv * along))
        actb[1, c, m] = (g + dinput).astype(BF)

        @pl.when(me_l > 0)
        def _():
            gather_there(1, m, me_l - 1)

        send(actb.at[1, c, m], actb.at[1, c, m], ac_s.at[1, m], ac_r.at[1, m], partner)
        racc[0:NE] = racc[0:NE] + dot(dl_hi, normed, TN) + dot(dl_lo, normed, TN)
        racc[NE:NE + 8] = racc[NE:NE + 8] + jnp.broadcast_to(
            jnp.sum(dnormed * x * inv, axis=0, keepdims=True), (8, H)
        )

    def place(k):
        backward = last * (k % 2) + (1 - last) * (k // NM)
        return backward, last * (k // 2) + (1 - last) * (k % NM)

    def step(k, carry):
        backward, m = place(k)
        before, n = place((k + 2 * NM - 1) % (2 * NM))

        @pl.when(backward == 0)
        def _():
            arrive(0, m)
            forward_compute(m)

        @pl.when(backward == 1)
        def _():
            arrive(1, m)
            backward_compute(m)

        late = (k > 0) & ((last == 1) | (k != NM))

        @pl.when(late & (before == 0))
        def _():
            forward_result(n)

        @pl.when(late & (before == 1))
        def _():
            backward_result(n)

        @pl.when(backward == 0)
        def _():
            forward_scatter(m)

        @pl.when(backward == 1)
        def _():
            backward_scatter(m)

        @pl.when((last == 0) & (k == NM - 1))
        def _():
            forward_result(NM - 1)

        return carry

    lax.fori_loop(0, 2 * NM, step, 0)
    backward_result(NM - 1)

    rgs[...] = racc[...]
    mine = c == me_y // (ND // 2)
    for j in range(ND // 2):
        yy = c * (ND // 2) + j
        src = rgs.at[:, pl.ds(j * DS, DS)]

        @pl.when(yy != me_y)
        def _():
            send(src, ybuf.at[me_y], r1_s.at[j], r1_r, {"dp": yy})

        @pl.when(yy == me_y)
        def _():
            copy(src, ybuf.at[me_y], r1_r)

    per = DS // NE

    @pl.when(mine)
    def _():
        wait(ybuf, r1_r)
        total = ybuf[0]
        for j in range(1, ND):
            total = total + ybuf[j]
        ysum[...] = total
        for k in range(NZ):
            for cc in range(2):
                ee = 2 * ((z + k) % NZ) + (c + cc) % 2
                src = ysum.at[:, pl.ds(pl.multiple_of(ee * per // 128 * 128, 128), 128)]
                if k == 0 and cc == 0:
                    copy(src, zbuf.at[z], r2_r)
                else:
                    send(src, zbuf.at[z], r2_s, r2_r, {"expert": ee})

    for m in range(NM):
        for i, ref in enumerate((hid, nsl, dga, dup, gsl)):
            if i in (1, 4):
                wait(ref.at[:, m], y_r.at[i, m])
            else:
                wait(ref.at[pl.ds(0, ND - 1), m], y_r.at[i, m])
    rows = ND * NM * R
    n_t = nsl[...].reshape(rows, DS)
    gg_ref[...] = dot(n_t, dga[...].reshape(rows, F), TN).astype(BF)
    ug_ref[...] = dot(n_t, dup[...].reshape(rows, F), TN).astype(BF)
    dg_ref[...] = dot(hid[...].reshape(rows, F), gsl[...].reshape(rows, DS), TN).astype(BF)

    wait(zbuf, r2_r)
    total = zbuf[0]
    for k in range(1, NZ):
        total = total + zbuf[k]
    rg_ref[...] = total

    for kind, out in enumerate((act_ref, igr_ref)):
        for m in range(NM):
            wait(actb.at[kind, oc, m], ac_r.at[kind, m])
            for half in range(2):
                v = actb[kind, half, m].astype(F32)
                v = v[:8] * mine0 + v[8:] * (1.0 - mine0)
                out[m, :, half * H:(half + 1) * H] = v.astype(BF)

    for kind in range(2):
        wait(ebr.at[kind], e_s.at[kind])
        for m in range(NM):
            wait(xall.at[kind, m, 0], fw_s.at[kind, m])
            wait(actb.at[kind, 0, m], ac_s.at[kind, m])
            sends = me_l < NP - 1 if kind == 0 else me_l > 0
            first = me_l == 0 if kind == 0 else last == 1

            @pl.when(sends)
            def _():
                wait(xall.at[kind, m, 0], ag_s.at[kind, m])

            @pl.when(first)
            def _():
                wait(xall.at[kind, m, 0, pl.ds(0, R - 16)], ag0_s.at[kind, m])

            p, r = ((ps_f, rf), (ps_b, rb))[kind]
            wait(p.at[m], pr_s.at[kind, m])
            wait(r.at[m, pl.ds(0, NZ - 1)], rs_s.at[kind, m])
    wait(pmall.at[pl.ds(0, NE - 1)], m_s)
    for m in range(NM):
        for i, ref in enumerate((hid, nsl, dga, dup, gsl)):
            wait(ref.at[pl.ds(0, ND - 1), m], y_s.at[i, m])
    for j in range(ND // 2):
        @pl.when(c * (ND // 2) + j != me_y)
        def _():
            wait(ybuf.at[0], r1_s.at[j])

    @pl.when(mine)
    def _():
        wait(zbuf, r2_s)
        wait(zbuf.at[pl.ds(0, NZ - 1)], r2_s)


def local(embedded, out_grad, norm_gain, router_weight, gate_weight, up_weight, down_weight, routing):
    NM, _, D = embedded.shape
    F = gate_weight.shape[-1]
    NE, ND, NP = lax.axis_size("expert"), lax.axis_size("dp"), lax.axis_size("pipe")
    NZ, H, R, DS = NE // 2, D // 2, NE * 8, D // ND
    HX = H + 128
    V = pl.BlockSpec(memory_space=pltpu.VMEM)
    A = pl.BlockSpec(memory_space=pl.ANY)

    def vm(*shape):
        return pltpu.VMEM(shape, BF)

    def vf(*shape):
        return pltpu.VMEM(shape, F32)

    sem = pltpu.SemaphoreType.DMA
    shape = jax.ShapeDtypeStruct
    act, igr, gg, ug, dg, rg = pl.pallas_call(
        functools.partial(kernel, (NM, D, F, NE, ND, NP)),
        name="moe_layers",
        in_specs=[V, V, V, V, V, A, A, A],
        out_specs=[V] * 6,
        out_shape=[
            shape((NM, 8, D), BF), shape((NM, 8, D), BF), shape((DS, F), BF), shape((DS, F), BF),
            shape((F, DS), BF), shape((NE + 8, 128), F32),
        ],
        scratch_shapes=[
            vm(D, F), vm(D, F), vm(F, D),
            vm(2, 2, NM, 16, H), vm(2, NM, 16, H), vm(2, NM, 16, H),
            vf(NE, NM, 8, 128),
            vm(2, NM, 2, R, H), vm(NM, 2, R, H),
            vf(NM, R, F), vf(NM, R, F), vm(NM, R, F),
            vf(NM, R, 128), vf(NM, R, 128), vf(NM, R, NE),
            vm(NM, R, H), vm(NM, R, H), vm(NM, R, HX), vm(NM, R, HX),
            vf(R, H), vf(R, HX), vm(NM, R, H), vm(NM, R, HX),
            vm(NM, NZ, 16, H), vm(NM, NZ, 16, HX), vm(2, 2, NM, 16, H),
            vm(ND, NM, R, DS), vm(ND, NM, R, DS), vm(ND, NM, R, F), vm(ND, NM, R, F), vm(ND, NM, R, F),
            vf(NE + 8, H), vf(NE + 8, H), vf(ND, NE + 8, DS), vf(NE + 8, DS), vf(NZ, NE + 8, 128),
            sem((3,)), sem((2,)), sem((2,)), sem, sem,
            sem((2, NM)), sem((2, NM)), sem((2, NM)), sem((2, NM)), sem((2, NM)),
            sem((2, NM)), sem((2, NM)), sem((2, NM)), sem((2, NM)), sem((2, NM)), sem((2, NM)),
            sem((5, NM)), sem((5, NM)), sem((ND // 2,)), sem, sem, sem,
        ],
        compiler_params=pltpu.CompilerParams(
            collective_id=0, has_side_effects=True, vmem_limit_bytes=58 * 2**20
        ),
    )(
        embedded, out_grad, routing[0], norm_gain, router_weight[0],
        gate_weight[0, 0], up_weight[0, 0], down_weight[0, 0],
    )
    per = DS // NE
    part = lax.dynamic_slice_in_dim(rg, lax.axis_index("expert") * per % 128, per, 1)
    return (
        act[None], igr[None], gg[None, None], ug[None, None], dg[None, None],
        part[:NE].T[None], part[NE][None],
    )


def solution(mesh):
    return jax.shard_map(
        local,
        mesh=mesh,
        in_specs=(
            P(None, ("dp", "expert"), None),
            P(None, ("dp", "expert"), None),
            P("pipe", None),
            P("pipe", None, None),
            P("pipe", "expert", None, None),
            P("pipe", "expert", None, None),
            P("pipe", "expert", None, None),
            P("pipe", None, ("dp", "expert"), None),
        ),
        out_specs=(
            P("pipe", None, ("dp", "expert"), None),
            P("pipe", None, ("dp", "expert"), None),
            P("pipe", "expert", "dp", None),
            P("pipe", "expert", "dp", None),
            P("pipe", "expert", None, "dp"),
            P("pipe", ("dp", "expert"), None),
            P("pipe", ("dp", "expert")),
        ),
        check_vma=False,
    )
```

```python
import functools

import jax
import jax.numpy as jnp
from jax import lax
from jax.experimental import pallas as pl
from jax.experimental.pallas import tpu as pltpu
from jax.sharding import PartitionSpec as P

EPSILON = 1e-06
MESH = pl.DeviceIdType.MESH
BF = jnp.bfloat16
F32 = jnp.float32
NN = (((1,), (0,)), ((), ()))
NT = (((1,), (1,)), ((), ()))
TN = (((0,), (0,)), ((), ()))


def dot(a, b, dims):
    return lax.dot_general(a, b, dims, preferred_element_type=F32)


def col(value):
    return jnp.sum(value, axis=-1, keepdims=True)


def kernel(
    sizes,
    emb_ref, og_ref, ids_ref, gain_ref, rw_ref, gate_hbm, up_hbm, down_hbm,
    act_ref, igr_ref, gg_ref, ug_ref, dg_ref, rg_ref,
    wg, wu, wd, ebs, ebr, src0, pmall, xall, nrm, gpre, upre, hidb, invs, wst, lgs,
    ps_f, pr_f, ps_b, pr_b, qo_f, qo_b, qf, qb, rf, rb, actb,
    nsl, gsl, hid, dga, dup, racc, rgs, ybuf, ysum, zbuf,
    w_sem, e_s, e_r, m_s, m_r, ag0_s, ag_s, ag_r, fw_s, fw_r, pr_s, pr_rs, rs_s, rs_r, ac_s, ac_r,
    y_s, y_r, r1_s, r1_r, r2_s, r2_r,
):
    NM, D, F, NE, ND, NP = sizes
    NZ, H, R, DS = NE // 2, D // 2, NE * 8, D // ND
    HX = H + 128
    me_y = lax.axis_index("dp")
    me_l = lax.axis_index("pipe")
    me_e = lax.axis_index("expert")
    z = me_e // 2
    c = me_e % 2
    oc = 1 - c
    partner = {"expert": me_e + 1 - 2 * c}
    own_rows = pl.ds(pl.multiple_of(z * 16, 16), 16)
    own_half = pl.ds(pl.multiple_of(c * H, H), H)
    other_half = pl.ds(pl.multiple_of(oc * H, H), H)
    last = (me_l + 1) // NP
    far_first = sorted(range(1, NZ), key=lambda k: (-min(k, NZ - k), k))

    def send(src, dst, ss, rs, dev):
        pltpu.make_async_remote_copy(
            src_ref=src, dst_ref=dst, send_sem=ss, recv_sem=rs, device_id=dev, device_id_type=MESH
        ).start()

    def copy(src, dst, sem):
        pltpu.make_async_copy(src, dst, sem).start()

    def wait(ref, sem):
        pltpu.make_async_copy(ref, ref, sem).wait()

    copy(gate_hbm, wg, w_sem.at[0])
    copy(up_hbm, wu, w_sem.at[1])
    copy(down_hbm, wd, w_sem.at[2])

    barrier = pltpu.get_barrier_semaphore()

    def hello(dev):
        pl.semaphore_signal(barrier, inc=1, device_id=dev, device_id_type=MESH)

    hello(partner)
    for k in range(1, NZ):
        for cc in range(2):
            hello({"expert": 2 * ((z + k) % NZ) + cc})
    for j in range(1, ND):
        hello({"dp": (me_y + j) % ND})
    for step in (1, NP - 1):
        for k in range(NZ):
            hello({"pipe": (me_l + step) % NP, "expert": 2 * ((z + k) % NZ) + c})

    mine0 = (c == 0).astype(F32)
    for kind, ref in enumerate((emb_ref, og_ref)):
        for m in range(NM):
            v = ref[m].astype(F32)
            blk = jnp.concatenate([v * mine0, v * (1.0 - mine0)], axis=0).astype(BF)
            ebs[kind, 0, m] = blk[:, :H]
            ebs[kind, 1, m] = blk[:, H:]
    lanes8 = lax.broadcasted_iota(jnp.int32, (8, 128), 1)
    for m in range(NM):
        ids = ids_ref[m]
        table = jnp.zeros((8, 128), F32)
        for k in range(ids.shape[1]):
            table = table + (ids[:, k:k + 1] == lanes8).astype(F32)
        pmall[me_e, m] = table
    racc[...] = jnp.zeros(racc.shape, F32)

    pl.semaphore_wait(barrier, 1 + 2 * (NZ - 1) + (ND - 1) + 2 * NZ)

    for kind in range(2):
        send(ebs.at[kind, oc], ebr.at[kind], e_s.at[kind], e_r.at[kind], partner)
    send(pmall.at[me_e], pmall.at[me_e], m_s, m_r, partner)
    for k in range(1, NZ):
        for cc in range(2):
            send(
                pmall.at[me_e], pmall.at[me_e], m_s, m_r, {"expert": 2 * ((z + k) % NZ) + cc}
            )

    def gather_here(kind, m):
        src = src0.at[kind, m]
        dst = xall.at[kind, m, c, own_rows]
        for k in far_first:
            send(src, dst, ag0_s.at[kind, m], ag_r.at[kind, m], {"expert": 2 * ((z + k) % NZ) + c})
        copy(src, dst, ag_r.at[kind, m])

    def gather_there(kind, m, section):
        for k in far_first + [0]:
            send(
                actb.at[kind, c, m], xall.at[kind, m, c, own_rows],
                ag_s.at[kind, m], ag_r.at[kind, m],
                {"pipe": section, "expert": 2 * ((z + k) % NZ) + c},
            )

    for kind in range(2):
        wait(ebr.at[kind], e_r.at[kind])
        for m in range(NM):
            src0[kind, m] = (
                ebs[kind, c, m].astype(F32) + ebr[kind, m].astype(F32)
            ).astype(BF)
        if kind == 0:
            @pl.when(me_l == 0)
            def _():
                gather_here(0, 0)
        else:
            @pl.when(last == 1)
            def _():
                for m in range(NM):
                    gather_here(1, m)

    wait(pmall.at[pl.ds(0, NE - 1)], m_r)
    wait(wg, w_sem.at[0])
    wait(wu, w_sem.at[1])
    wait(wd, w_sem.at[2])

    def arrive(kind, m):
        wait(xall.at[kind, m, c], ag_r.at[kind, m])
        send(
            xall.at[kind, m, c], xall.at[kind, m, c], fw_s.at[kind, m], fw_r.at[kind, m], partner
        )
        wait(xall.at[kind, m, oc], fw_r.at[kind, m])

    lane_e = lax.broadcasted_iota(jnp.int32, (R, NE), 1)
    lane_x = lax.broadcasted_iota(jnp.int32, (R, 128), 1)

    def forward_compute(m):
        x0 = xall[0, m, 0].astype(F32)
        x1 = xall[0, m, 1].astype(F32)
        inv = lax.rsqrt((col(x0 * x0) + col(x1 * x1)) * (1.0 / D) + EPSILON)
        n0 = (x0 * inv * gain_ref[0:1, :H]).astype(BF)
        n1 = (x1 * inv * gain_ref[0:1, H:]).astype(BF)
        nrm[m, 0] = n0
        nrm[m, 1] = n1
        logits = dot(n0, rw_ref[:, :H], NT) + dot(n1, rw_ref[:, H:], NT)
        named = pmall[:, m].reshape(R, 128)[:, :NE]
        chosen = named * jax.nn.sigmoid(logits)
        w = col(jnp.where(lane_e == me_e, chosen, 0.0)) / col(chosen)
        invs[m] = jnp.broadcast_to(inv, (R, 128))
        wst[m] = jnp.broadcast_to(w, (R, 128))
        lgs[m] = logits
        a = dot(n0, wg[:H, :], NN) + dot(n1, wg[H:, :], NN)
        b = dot(n0, wu[:H, :], NN) + dot(n1, wu[H:, :], NN)
        gpre[m] = a
        upre[m] = b
        h = (a * jax.nn.sigmoid(a) * b).astype(BF)
        hidb[m] = h
        hid[me_y, m] = (h.astype(F32) * w).astype(BF)
        ps_f[m] = (dot(h, wd[:, other_half], NN) * w).astype(BF)
        send(ps_f.at[m], pr_f.at[m], pr_s.at[0, m], pr_rs.at[0, m], partner)
        qo_f[m] = dot(h, wd[:, own_half], NN) * w

    def scatter(kind, m, q, r):
        for k in far_first:
            zz = (z + k) % NZ
            send(
                q.at[m, pl.ds(pl.multiple_of(zz * 16, 16), 16)], r.at[m, z],
                rs_s.at[kind, m], rs_r.at[kind, m], {"expert": 2 * zz + c},
            )
        copy(q.at[m, own_rows], r.at[m, z], rs_r.at[kind, m])

    def half_slice(ref, yy):
        start = yy * DS
        return ref.at[start // H, :, pl.ds(pl.multiple_of(start % H, 128), DS)]

    def to_replicas(m, whole, halves, slices, base):
        for j in range(1, ND):
            yy = (me_y + j) % ND
            for i, ref in enumerate(whole):
                send(
                    ref.at[me_y, m], ref.at[me_y, m], y_s.at[base + i, m], y_r.at[base + i, m],
                    {"dp": yy},
                )
            i = base + len(whole)
            send(half_slice(halves, yy), slices.at[me_y, m], y_s.at[i, m], y_r.at[i, m], {"dp": yy})
        i = base + len(whole)
        copy(half_slice(halves, me_y), slices.at[me_y, m], y_r.at[i, m])

    def forward_scatter(m):
        wait(pr_f.at[m], pr_rs.at[0, m])
        qf[m] = (qo_f[m] + pr_f[m].astype(F32)).astype(BF)
        scatter(0, m, qf, rf)

        @pl.when((me_l == 0) & (m < NM - 1))
        def _():
            gather_here(0, m + 1)

        to_replicas(m, (hid,), nrm.at[m], nsl, 0)

    def forward_result(m):
        wait(rf.at[m], rs_r.at[0, m])
        total = xall[0, m, c, own_rows].astype(F32)
        for k in range(NZ):
            total = total + rf[m, k].astype(F32)
        actb[0, c, m] = total.astype(BF)

        @pl.when(last == 0)
        def _():
            gather_there(0, m, me_l + 1)

        send(actb.at[0, c, m], actb.at[0, c, m], ac_s.at[0, m], ac_r.at[0, m], partner)

    def backward_compute(m):
        dh = dot(xall[1, m, 0], wd[:, :H], NT) + dot(xall[1, m, 1], wd[:, H:], NT)
        w = wst[m][:, :1]
        a = gpre[m]
        b = upre[m]
        dw = col(dh * hidb[m].astype(F32))
        dhw = dh * w
        s = jax.nn.sigmoid(a)
        dgate = (dhw * b * s * (1.0 + a * (1.0 - s))).astype(BF)
        dupv = (dhw * (a * s)).astype(BF)
        dga[me_y, m] = dgate
        dup[me_y, m] = dupv
        sv = col(dgate.astype(F32) * a + dupv.astype(F32) * b)
        dw_hi = dw.astype(BF).astype(F32)
        sv_hi = sv.astype(BF).astype(F32)
        ext = jnp.where(lane_x == me_e, dw_hi, 0.0)
        ext = jnp.where(lane_x == NE + me_e, dw - dw_hi, ext)
        ext = jnp.where(lane_x == 2 * NE + me_e, sv_hi, ext)
        ext = jnp.where(lane_x == 3 * NE + me_e, sv - sv_hi, ext)
        ps_b[m, :, :H] = (
            dot(dgate, wg[other_half, :], NT) + dot(dupv, wu[other_half, :], NT)
        ).astype(BF)
        ps_b[m, :, H:] = ext.astype(BF)
        send(ps_b.at[m], pr_b.at[m], pr_s.at[1, m], pr_rs.at[1, m], partner)
        qo_b[:, :H] = dot(dgate, wg[own_half, :], NT) + dot(dupv, wu[own_half, :], NT)
        qo_b[:, H:] = ext

    def backward_scatter(m):
        wait(pr_b.at[m], pr_rs.at[1, m])
        qb[m] = (qo_b[...] + pr_b[m].astype(F32)).astype(BF)
        scatter(1, m, qb, rb)
        to_replicas(m, (dga, dup), xall.at[1, m], gsl, 2)

    def backward_result(m):
        wait(rb.at[m], rs_r.at[1, m])
        total = rb[m, 0].astype(F32)
        for k in range(1, NZ):
            total = total + rb[m, k].astype(F32)
        ext = total[:, H:]
        dw = ext[:, :NE] + ext[:, NE:2 * NE]
        sv = col(ext[:, 2 * NE:3 * NE] + ext[:, 3 * NE:4 * NE])
        logits = lgs[m, own_rows]
        named = pmall[pl.ds(2 * z, 2), m].reshape(16, 128)[:, :NE]
        chosen = named * jax.nn.sigmoid(logits)
        prob_total = col(chosen)
        weights = chosen / prob_total
        dchosen = (dw - col(dw * weights)) / prob_total
        dlogits = dchosen * chosen * (1.0 - chosen)
        dl_hi = dlogits.astype(BF)
        dl_lo = (dlogits - dl_hi.astype(F32)).astype(BF)
        router_half = rw_ref[:, own_half]
        dnormed = total[:, :H] + dot(dl_hi, router_half, NN) + dot(dl_lo, router_half, NN)
        inv = invs[m, own_rows][:, :1]
        gain_half = gain_ref[0:1, own_half]
        x = xall[0, m, c, own_rows].astype(F32)
        g = xall[1, m, c, own_rows].astype(F32)
        normed = nrm[m, c, own_rows]
        along = (sv + col(dlogits * logits)) * (1.0 / D)
        dinput = inv * (dnormed * gain_half - x * (inv * along))
        actb[1, c, m] = (g + dinput).astype(BF)

        @pl.when(me_l > 0)
        def _():
            gather_there(1, m, me_l - 1)

        send(actb.at[1, c, m], actb.at[1, c, m], ac_s.at[1, m], ac_r.at[1, m], partner)
        racc[0:NE] = racc[0:NE] + dot(dl_hi, normed, TN) + dot(dl_lo, normed, TN)
        racc[NE:NE + 8] = racc[NE:NE + 8] + jnp.broadcast_to(
            jnp.sum(dnormed * x * inv, axis=0, keepdims=True), (8, H)
        )

    def step(k, carry):
        end = k // (2 * NM)
        back = last * (k % 2) + (1 - last) * (k // NM)
        m = last * (k // 2) + (1 - last) * (k % NM)

        @pl.when((back == 0) & (end == 0))
        def _():
            arrive(0, m)
            forward_compute(m)

        @pl.when((back == 1) & (end == 0))
        def _():
            arrive(1, m)
            backward_compute(m)
            backward_scatter(m)

        after = (last == 1) & (k > 2 * NM)

        @pl.when(((last == 0) & (back == 0) & (end == 0)) | after)
        def _():
            n = m * (1 - last) + (k - 2 * NM - 1) * last
            forward_scatter(n)
            forward_result(n)

        inner = (last == 1) & (back == 0) & (k > 0) & (k <= 2 * NM)

        @pl.when(((last == 0) & (back == 1) & (end == 0)) | inner)
        def _():
            backward_result(m - last)

        return carry

    lax.fori_loop(0, 3 * NM + 1, step, 0)

    rgs[...] = racc[...]
    mine = c == me_y // (ND // 2)
    for j in range(ND // 2):
        yy = c * (ND // 2) + j
        src = rgs.at[:, pl.ds(j * DS, DS)]

        @pl.when(yy != me_y)
        def _():
            send(src, ybuf.at[me_y], r1_s.at[j], r1_r, {"dp": yy})

        @pl.when(yy == me_y)
        def _():
            copy(src, ybuf.at[me_y], r1_r)

    per = DS // NE

    @pl.when(mine)
    def _():
        wait(ybuf, r1_r)
        total = ybuf[0]
        for j in range(1, ND):
            total = total + ybuf[j]
        ysum[...] = total
        for k in range(NZ):
            for cc in range(2):
                ee = 2 * ((z + k) % NZ) + (c + cc) % 2
                src = ysum.at[:, pl.ds(pl.multiple_of(ee * per // 128 * 128, 128), 128)]
                if k == 0 and cc == 0:
                    copy(src, zbuf.at[z], r2_r)
                else:
                    send(src, zbuf.at[z], r2_s, r2_r, {"expert": ee})

    for m in range(NM):
        for i, ref in enumerate((hid, nsl, dga, dup, gsl)):
            if i in (1, 4):
                wait(ref.at[:, m], y_r.at[i, m])
            else:
                wait(ref.at[pl.ds(0, ND - 1), m], y_r.at[i, m])
    rows = ND * NM * R
    n_t = nsl[...].reshape(rows, DS)
    gg_ref[...] = dot(n_t, dga[...].reshape(rows, F), TN).astype(BF)
    ug_ref[...] = dot(n_t, dup[...].reshape(rows, F), TN).astype(BF)
    dg_ref[...] = dot(hid[...].reshape(rows, F), gsl[...].reshape(rows, DS), TN).astype(BF)

    wait(zbuf, r2_r)
    total = zbuf[0]
    for k in range(1, NZ):
        total = total + zbuf[k]
    rg_ref[...] = total

    for kind, out in enumerate((act_ref, igr_ref)):
        for m in range(NM):
            wait(actb.at[kind, oc, m], ac_r.at[kind, m])
            for half in range(2):
                v = actb[kind, half, m].astype(F32)
                v = v[:8] * mine0 + v[8:] * (1.0 - mine0)
                out[m, :, half * H:(half + 1) * H] = v.astype(BF)

    for kind in range(2):
        wait(ebr.at[kind], e_s.at[kind])
        for m in range(NM):
            wait(xall.at[kind, m, 0], fw_s.at[kind, m])
            wait(actb.at[kind, 0, m], ac_s.at[kind, m])
            sends = me_l < NP - 1 if kind == 0 else me_l > 0
            first = me_l == 0 if kind == 0 else last == 1

            @pl.when(sends)
            def _():
                wait(xall.at[kind, m, 0], ag_s.at[kind, m])

            @pl.when(first)
            def _():
                wait(xall.at[kind, m, 0, pl.ds(0, R - 16)], ag0_s.at[kind, m])

            p, r = ((ps_f, rf), (ps_b, rb))[kind]
            wait(p.at[m], pr_s.at[kind, m])
            wait(r.at[m, pl.ds(0, NZ - 1)], rs_s.at[kind, m])
    wait(pmall.at[pl.ds(0, NE - 1)], m_s)
    for m in range(NM):
        for i, ref in enumerate((hid, nsl, dga, dup, gsl)):
            wait(ref.at[pl.ds(0, ND - 1), m], y_s.at[i, m])
    for j in range(ND // 2):
        @pl.when(c * (ND // 2) + j != me_y)
        def _():
            wait(ybuf.at[0], r1_s.at[j])

    @pl.when(mine)
    def _():
        wait(zbuf, r2_s)
        wait(zbuf.at[pl.ds(0, NZ - 1)], r2_s)


def local(embedded, out_grad, norm_gain, router_weight, gate_weight, up_weight, down_weight, routing):
    NM, _, D = embedded.shape
    F = gate_weight.shape[-1]
    NE, ND, NP = lax.axis_size("expert"), lax.axis_size("dp"), lax.axis_size("pipe")
    NZ, H, R, DS = NE // 2, D // 2, NE * 8, D // ND
    HX = H + 128
    V = pl.BlockSpec(memory_space=pltpu.VMEM)
    A = pl.BlockSpec(memory_space=pl.ANY)

    def vm(*shape):
        return pltpu.VMEM(shape, BF)

    def vf(*shape):
        return pltpu.VMEM(shape, F32)

    sem = pltpu.SemaphoreType.DMA
    shape = jax.ShapeDtypeStruct
    act, igr, gg, ug, dg, rg = pl.pallas_call(
        functools.partial(kernel, (NM, D, F, NE, ND, NP)),
        name="moe_layers",
        in_specs=[V, V, V, V, V, A, A, A],
        out_specs=[V] * 6,
        out_shape=[
            shape((NM, 8, D), BF), shape((NM, 8, D), BF), shape((DS, F), BF), shape((DS, F), BF),
            shape((F, DS), BF), shape((NE + 8, 128), F32),
        ],
        scratch_shapes=[
            vm(D, F), vm(D, F), vm(F, D),
            vm(2, 2, NM, 16, H), vm(2, NM, 16, H), vm(2, NM, 16, H),
            vf(NE, NM, 8, 128),
            vm(2, NM, 2, R, H), vm(NM, 2, R, H),
            vf(NM, R, F), vf(NM, R, F), vm(NM, R, F),
            vf(NM, R, 128), vf(NM, R, 128), vf(NM, R, NE),
            vm(NM, R, H), vm(NM, R, H), vm(NM, R, HX), vm(NM, R, HX),
            vf(NM, R, H), vf(R, HX), vm(NM, R, H), vm(NM, R, HX),
            vm(NM, NZ, 16, H), vm(NM, NZ, 16, HX), vm(2, 2, NM, 16, H),
            vm(ND, NM, R, DS), vm(ND, NM, R, DS), vm(ND, NM, R, F), vm(ND, NM, R, F), vm(ND, NM, R, F),
            vf(NE + 8, H), vf(NE + 8, H), vf(ND, NE + 8, DS), vf(NE + 8, DS), vf(NZ, NE + 8, 128),
            sem((3,)), sem((2,)), sem((2,)), sem, sem,
            sem((2, NM)), sem((2, NM)), sem((2, NM)), sem((2, NM)), sem((2, NM)),
            sem((2, NM)), sem((2, NM)), sem((2, NM)), sem((2, NM)), sem((2, NM)), sem((2, NM)),
            sem((5, NM)), sem((5, NM)), sem((ND // 2,)), sem, sem, sem,
        ],
        compiler_params=pltpu.CompilerParams(
            collective_id=0, has_side_effects=True, vmem_limit_bytes=58 * 2**20
        ),
    )(
        embedded, out_grad, routing[0], norm_gain, router_weight[0].T,
        gate_weight[0, 0], up_weight[0, 0], down_weight[0, 0],
    )
    per = DS // NE
    part = lax.dynamic_slice_in_dim(rg, lax.axis_index("expert") * per % 128, per, 1)
    return (
        act[None], igr[None], gg[None, None], ug[None, None], dg[None, None],
        part[:NE].T[None], part[NE][None],
    )


def solution(mesh):
    return jax.shard_map(
        local,
        mesh=mesh,
        in_specs=(
            P(None, ("dp", "expert"), None),
            P(None, ("dp", "expert"), None),
            P("pipe", None),
            P("pipe", None, None),
            P("pipe", "expert", None, None),
            P("pipe", "expert", None, None),
            P("pipe", "expert", None, None),
            P("pipe", None, ("dp", "expert"), None),
        ),
        out_specs=(
            P("pipe", None, ("dp", "expert"), None),
            P("pipe", None, ("dp", "expert"), None),
            P("pipe", "expert", "dp", None),
            P("pipe", "expert", "dp", None),
            P("pipe", "expert", None, "dp"),
            P("pipe", ("dp", "expert"), None),
            P("pipe", ("dp", "expert")),
        ),
        check_vma=False,
    )
```

```python
import functools

import jax
import jax.numpy as jnp
from jax import lax
from jax.experimental import pallas as pl
from jax.experimental.pallas import tpu as pltpu
from jax.sharding import PartitionSpec as P

EPSILON = 1e-06
MESH = pl.DeviceIdType.MESH
BF = jnp.bfloat16
F32 = jnp.float32
NN = (((1,), (0,)), ((), ()))
NT = (((1,), (1,)), ((), ()))
TN = (((0,), (0,)), ((), ()))


def dot(a, b, dims):
    return lax.dot_general(a, b, dims, preferred_element_type=F32)


def col(value):
    return jnp.sum(value, axis=-1, keepdims=True)


def fold(value):
    half = value.shape[1] // 2
    return jnp.concatenate([value[:, :half], value[:, half:]], axis=0)


def twice(value):
    return jnp.concatenate([value, value], axis=0)


def kernel(
    sizes,
    emb_ref, og_ref, ids_ref, gain_ref, rw_ref, gate_hbm, up_hbm, down_hbm,
    act_ref, igr_ref, gg_ref, ug_ref, dg_ref, rg_ref,
    wg, wu, wd, ebs, src0, pmall, xall, nrm, gfull, gpre, upre, hidb, invs, wst, lgs,
    ps_f, pr_f, ps_b, pr_b, qo_f, qo_b, qf, qb, rf, rb, actb,
    nsl, gsl, hid, dgu, racc, rgs, ybuf, ysum, zbuf,
    w_sem, e_s, e_r, m_s, m_r, ag0_s, ag_s, ag_r, fw_s, fw_r, pr_s, pr_rs, rs_s, rs_r, ac_s, ac_r,
    y_s, y_r, yd_s, yd_r, yf_s, yf_r, r1_s, r1_r, r2_s, r2_r,
):
    NM, D, F, NE, ND, NP = sizes
    NZ, H, Q, R, DS = NE // 2, D // 2, D // 4, NE * 4, D // ND
    QX = Q + 128
    me_y = lax.axis_index("dp")
    me_l = lax.axis_index("pipe")
    me_e = lax.axis_index("expert")
    z = me_e // 2
    c = me_e % 2
    oc = 1 - c
    partner = {"expert": me_e + 1 - 2 * c}
    own_rows = pl.ds(pl.multiple_of(z * 16, 16), 16)
    own_tokens = pl.ds(pl.multiple_of(z * 8, 8), 8)
    own_half = pl.ds(pl.multiple_of(c * H, H), H)
    other_half = pl.ds(pl.multiple_of(oc * H, H), H)
    last = (me_l + 1) // NP
    far_first = sorted(range(1, NZ), key=lambda k: (-min(k, NZ - k), k))
    y_up, y_down = (me_y + 1) % ND, (me_y + ND - 1) % ND

    def send(src, dst, ss, rs, dev):
        pltpu.make_async_remote_copy(
            src_ref=src, dst_ref=dst, send_sem=ss, recv_sem=rs, device_id=dev, device_id_type=MESH
        ).start()

    def copy(src, dst, sem):
        pltpu.make_async_copy(src, dst, sem).start()

    def wait(ref, sem):
        pltpu.make_async_copy(ref, ref, sem).wait()

    copy(gate_hbm, wg, w_sem.at[0])
    copy(up_hbm, wu, w_sem.at[1])
    copy(down_hbm, wd, w_sem.at[2])

    barrier = pltpu.get_barrier_semaphore()

    def hello(dev):
        pl.semaphore_signal(barrier, inc=1, device_id=dev, device_id_type=MESH)

    hello(partner)
    for k in range(1, NZ):
        for cc in range(2):
            hello({"expert": 2 * ((z + k) % NZ) + cc})
    for j in range(1, ND):
        hello({"dp": (me_y + j) % ND})
    for step in (1, NP - 1):
        for k in range(NZ):
            hello({"pipe": (me_l + step) % NP, "expert": 2 * ((z + k) % NZ) + c})

    mine0 = (c == 0).astype(F32)
    for kind, ref in enumerate((emb_ref, og_ref)):
        for m in range(NM):
            v = ref[m].astype(F32)
            low, high = v[:, :H], v[:, H:]
            src0[kind, c, m] = fold(low * mine0 + high * (1.0 - mine0)).astype(BF)
            ebs[kind, m] = fold(high * mine0 + low * (1.0 - mine0)).astype(BF)
    lanes8 = lax.broadcasted_iota(jnp.int32, (8, 128), 1)
    for m in range(NM):
        ids = ids_ref[m]
        table = jnp.zeros((8, 128), F32)
        for k in range(ids.shape[1]):
            table = table + (ids[:, k:k + 1] == lanes8).astype(F32)
        pmall[c * NZ + z, m] = table
    racc[...] = jnp.zeros(racc.shape, F32)

    pl.semaphore_wait(barrier, 1 + 2 * (NZ - 1) + (ND - 1) + 2 * NZ)

    for kind in range(2):
        send(ebs.at[kind], src0.at[kind, c], e_s.at[kind], e_r.at[kind], partner)
    my_table = pmall.at[c * NZ + z]
    send(my_table, my_table, m_s, m_r, partner)
    for k in range(1, NZ):
        for cc in range(2):
            send(my_table, my_table, m_s, m_r, {"expert": 2 * ((z + k) % NZ) + cc})

    def gather_here(kind, m, s):
        src = src0.at[kind, s, m]
        dst = xall.at[kind, m, s, c, own_rows]
        for k in far_first:
            send(
                src, dst, ag0_s.at[kind, m, s], ag_r.at[kind, m, s],
                {"expert": 2 * ((z + k) % NZ) + c},
            )
        copy(src, dst, ag_r.at[kind, m, s])

    def gather_there(kind, m, s, section):
        for k in far_first + [0]:
            send(
                actb.at[kind, c, m, s], xall.at[kind, m, s, c, own_rows],
                ag_s.at[kind, m, s], ag_r.at[kind, m, s],
                {"pipe": section, "expert": 2 * ((z + k) % NZ) + c},
            )

    wait(src0.at[0, oc], e_r.at[0])

    @pl.when(me_l == 0)
    def _():
        for s in range(2):
            gather_here(0, 0, s)

    wait(src0.at[1, oc], e_r.at[1])

    @pl.when(last == 1)
    def _():
        for m in range(NM):
            for s in range(2):
                gather_here(1, m, s)

    wait(pmall.at[pl.ds(0, NE - 1)], m_r)
    wait(wg, w_sem.at[0])
    wait(wu, w_sem.at[1])
    wait(wd, w_sem.at[2])

    def arrive(kind, m, s):
        got = xall.at[kind, m, s, c]
        wait(got, ag_r.at[kind, m, s])
        send(got, got, fw_s.at[kind, m, s], fw_r.at[kind, m, s], partner)
        wait(xall.at[kind, m, s, oc], fw_r.at[kind, m, s])

    def quarters(kind, m, s):
        out = []
        for half in range(2):
            v = xall[kind, m, s, half].astype(F32).reshape(NZ, 2, 8, Q)
            out += [v[:, 0].reshape(R, Q), v[:, 1].reshape(R, Q)]
        return out

    lane_e = lax.broadcasted_iota(jnp.int32, (R, NE), 1)
    lane_x = lax.broadcasted_iota(jnp.int32, (R, 128), 1)

    def forward_compute(m, s):
        xs = quarters(0, m, s)
        square = xs[0] * xs[0]
        for v in xs[1:]:
            square = square + v * v
        inv = lax.rsqrt(col(square) * (1.0 / D) + EPSILON)
        for i, v in enumerate(xs):
            nrm[m, s, :, i * Q:(i + 1) * Q] = (v * inv * gain_ref[0:1, i * Q:(i + 1) * Q]).astype(BF)
        normed = nrm[m, s]
        logits = dot(normed, rw_ref[...], NT)
        named = pmall[s * NZ:(s + 1) * NZ, m].reshape(R, 128)[:, :NE]
        chosen = named * jax.nn.sigmoid(logits)
        w = col(jnp.where(lane_e == me_e, chosen, 0.0)) / col(chosen)
        invs[m, s] = jnp.broadcast_to(inv, (R, 128))
        wst[m, s] = jnp.broadcast_to(w, (R, 128))
        lgs[m, s] = logits
        a = dot(normed, wg[...], NN)
        b = dot(normed, wu[...], NN)
        gpre[m, s] = a
        upre[m, s] = b
        h = (a * jax.nn.sigmoid(a) * b).astype(BF)
        hidb[m, s] = h
        hid[me_y, m, s] = (h.astype(F32) * w).astype(BF)
        ps_f[m, s] = (dot(h, wd[:, other_half], NN) * w).astype(BF)
        send(ps_f.at[m, s], pr_f.at[m, s], pr_s.at[0, m, s], pr_rs.at[0, m, s], partner)
        qo_f[m, s] = dot(h, wd[:, own_half], NN) * w

    def scatter(kind, m, s, q, r):
        for k in far_first:
            zz = (z + k) % NZ
            send(
                q.at[m, s, pl.ds(pl.multiple_of(zz * 16, 16), 16)], r.at[m, s, z],
                rs_s.at[kind, m, s], rs_r.at[kind, m, s], {"expert": 2 * zz + c},
            )
        copy(q.at[m, s, own_rows], r.at[m, s, z], rs_r.at[kind, m, s])

    def part(ref, yy):
        return ref.at[:, pl.ds(pl.multiple_of(yy * DS, DS), DS)]

    def folded(v):
        width = v.shape[1] // 2
        low, high = v[:, :width].reshape(NZ, 1, 8, width), v[:, width:].reshape(NZ, 1, 8, width)
        return jnp.concatenate([low, high], axis=1).reshape(NZ * 16, width)

    def forward_scatter(m, s):
        wait(pr_f.at[m, s], pr_rs.at[0, m, s])
        qf[m, s] = folded(qo_f[m, s] + pr_f[m, s].astype(F32)).astype(BF)
        scatter(0, m, s, qf, rf)

        @pl.when((me_l == 0) & (m < NM - 1))
        def _():
            gather_here(0, m + 1, s)

    def forward_replicas(m, s):
        for j in range(1, ND):
            yy = (me_y + j) % ND
            mine = hid.at[me_y, m, s]
            send(mine, mine, y_s.at[0, m], y_r.at[0, m], {"dp": yy})
            send(part(nrm.at[m, s], yy), nsl.at[me_y, m, s], y_s.at[1, m], y_r.at[1, m], {"dp": yy})
        copy(part(nrm.at[m, s], me_y), nsl.at[me_y, m, s], y_r.at[1, m])

    def keep(kind, m, s):
        block = actb.at[kind, c, m, s]

        @pl.when(oc == s)
        def _():
            send(block, block, ac_s.at[kind, m], ac_r.at[kind, m], partner)

    def forward_result(m, s):
        wait(rf.at[m, s], rs_r.at[0, m, s])
        total = xall[0, m, s, c, own_rows].astype(F32)
        for k in range(NZ):
            total = total + rf[m, s, k].astype(F32)
        actb[0, c, m, s] = total.astype(BF)

        @pl.when(last == 0)
        def _():
            gather_there(0, m, s, me_l + 1)

        keep(0, m, s)

    def backward_compute(m, s):
        for i, v in enumerate(quarters(1, m, s)):
            gfull[m, s, :, i * Q:(i + 1) * Q] = v.astype(BF)
        dh = dot(gfull[m, s], wd[...], NT)
        w = wst[m, s][:, :1]
        a = gpre[m, s]
        b = upre[m, s]
        dw = col(dh * hidb[m, s].astype(F32))
        dhw = dh * w
        sg = jax.nn.sigmoid(a)
        dgate = (dhw * b * sg * (1.0 + a * (1.0 - sg))).astype(BF)
        dupv = (dhw * (a * sg)).astype(BF)
        dgu[me_y, m, s, 0] = dgate
        dgu[me_y, m, s, 1] = dupv
        sv = col(dgate.astype(F32) * a + dupv.astype(F32) * b)
        dw_hi = dw.astype(BF).astype(F32)
        sv_hi = sv.astype(BF).astype(F32)
        ext = jnp.where(lane_x == me_e, dw_hi, 0.0)
        ext = jnp.where(lane_x == NE + me_e, dw - dw_hi, ext)
        ext = jnp.where(lane_x == 2 * NE + me_e, sv_hi, ext)
        ext = jnp.where(lane_x == 3 * NE + me_e, sv - sv_hi, ext)
        ps_b[m, s, :, :H] = (
            dot(dgate, wg[other_half, :], NT) + dot(dupv, wu[other_half, :], NT)
        ).astype(BF)
        ps_b[m, s, :, H:] = ext.astype(BF)
        send(ps_b.at[m, s], pr_b.at[m, s], pr_s.at[1, m, s], pr_rs.at[1, m, s], partner)
        qo_b[:, :H] = dot(dgate, wg[own_half, :], NT) + dot(dupv, wu[own_half, :], NT)
        qo_b[:, H:] = ext

    def backward_scatter(m, s):
        wait(pr_b.at[m, s], pr_rs.at[1, m, s])
        q = qo_b[...] + pr_b[m, s].astype(F32)
        qb[m, s, :, :Q] = folded(q[:, :H]).astype(BF)
        ext = q[:, H:].reshape(NZ, 1, 8, 128)
        qb[m, s, :, Q:] = (
            jnp.concatenate([ext, jnp.zeros_like(ext)], axis=1).reshape(NZ * 16, 128).astype(BF)
        )
        scatter(1, m, s, qb, rb)

    def backward_replicas(m, s):
        mine = dgu.at[me_y, m, s]
        send(mine, mine, yd_s.at[0, m, s], yd_r.at[0, m, s], {"dp": y_up})
        send(mine, mine, yd_s.at[1, m, s], yd_r.at[1, m, s], {"dp": y_down})
        for j in range(1, ND):
            yy = (me_y + j) % ND
            send(part(gfull.at[m, s], yy), gsl.at[me_y, m, s], y_s.at[2, m], y_r.at[2, m], {"dp": yy})
        copy(part(gfull.at[m, s], me_y), gsl.at[me_y, m, s], y_r.at[2, m])

    def pass_on(m):
        for s, source, target in ((0, y_down, y_up), (1, y_up, y_down)):
            block = dgu.at[source, m, s]
            wait(block, yd_r.at[s, m, s])
            send(block, block, yf_s.at[m, s], yf_r.at[m, s], {"dp": target})

    def backward_result(m, s):
        wait(rb.at[m, s], rs_r.at[1, m, s])
        total = rb[m, s, 0].astype(F32)
        for k in range(1, NZ):
            total = total + rb[m, s, k].astype(F32)
        ext = total[:8, Q:]
        dw = ext[:, :NE] + ext[:, NE:2 * NE]
        sv = col(ext[:, 2 * NE:3 * NE] + ext[:, 3 * NE:4 * NE])
        logits = lgs[m, s, own_tokens]
        named = pmall[s * NZ + z, m][:, :NE]
        chosen = named * jax.nn.sigmoid(logits)
        prob_total = col(chosen)
        weights = chosen / prob_total
        dchosen = (dw - col(dw * weights)) / prob_total
        dlogits = dchosen * chosen * (1.0 - chosen)
        dl_hi = dlogits.astype(BF).astype(F32)
        dl = jnp.concatenate([dl_hi, dlogits - dl_hi], axis=0).astype(BF)
        term = dot(dl, rw_ref[:, own_half], NN)
        dnormed = total[:, :Q] + fold(term[:8] + term[8:])
        inv = twice(invs[m, s, own_tokens][:, :1])
        gain_row = gain_ref[0:1, own_half]
        gain = jnp.concatenate(
            [jnp.broadcast_to(gain_row[:, :Q], (8, Q)), jnp.broadcast_to(gain_row[:, Q:], (8, Q))],
            axis=0,
        )
        x = xall[0, m, s, c, own_rows].astype(F32)
        g = xall[1, m, s, c, own_rows].astype(F32)
        along = twice((sv + col(dlogits * logits)) * (1.0 / D))
        dinput = inv * (dnormed * gain - x * (inv * along))
        actb[1, c, m, s] = (g + dinput).astype(BF)

        @pl.when(me_l > 0)
        def _():
            gather_there(1, m, s, me_l - 1)

        keep(1, m, s)
        normed = x * inv * gain
        gained = dnormed * x * inv
        for i in range(2):
            rows = slice(8 * i, 8 * i + 8)
            cols = slice(Q * i, Q * i + Q)
            racc[0:NE, cols] = racc[0:NE, cols] + dot(dl, twice(normed[rows]).astype(BF), TN)
            racc[NE:NE + 8, cols] = racc[NE:NE + 8, cols] + gained[rows]

    def step(k, carry):
        m = k % NM
        first = k < NM
        is_last = last == 1
        forward = (first & (last == 0)) | ((k >= NM) & is_last)
        backward = ((k >= NM) & (last == 0)) | (first & is_last)
        for s in range(2):
            @pl.when(first)
            def _():
                arrive(0, m, s)
                forward_compute(m, s)

            @pl.when(forward)
            def _():
                forward_scatter(m, s)

            @pl.when(backward)
            def _():
                arrive(1, m, s)
                backward_compute(m, s)
                backward_scatter(m, s)
                backward_replicas(m, s)

            @pl.when(first)
            def _():
                forward_replicas(m, s)

        @pl.when(backward & (m > 0))
        def _():
            pass_on(m - 1)

        for s in range(2):
            @pl.when(forward)
            def _():
                forward_result(m, s)

            @pl.when(backward)
            def _():
                backward_result(m, s)

        return carry

    lax.fori_loop(0, 2 * NM, step, 0)
    pass_on(NM - 1)

    rgs[0:NE] = racc[0:NE]
    rgs[NE:NE + 8] = jnp.broadcast_to(
        jnp.sum(racc[NE:NE + 8], axis=0, keepdims=True), (8, H)
    )
    mine = c == me_y // (ND // 2)
    for j in range(ND // 2):
        yy = c * (ND // 2) + j
        src = rgs.at[:, pl.ds(j * DS, DS)]

        @pl.when(yy != me_y)
        def _():
            send(src, ybuf.at[me_y], r1_s.at[j], r1_r, {"dp": yy})

        @pl.when(yy == me_y)
        def _():
            copy(src, ybuf.at[me_y], r1_r)

    per = DS // NE

    @pl.when(mine)
    def _():
        wait(ybuf, r1_r)
        total = ybuf[0]
        for j in range(1, ND):
            total = total + ybuf[j]
        ysum[...] = total
        for k in range(NZ):
            for cc in range(2):
                ee = 2 * ((z + k) % NZ) + (c + cc) % 2
                src = ysum.at[:, pl.ds(pl.multiple_of(ee * per // 128 * 128, 128), 128)]
                if k == 0 and cc == 0:
                    copy(src, zbuf.at[z], r2_r)
                else:
                    send(src, zbuf.at[z], r2_s, r2_r, {"expert": ee})

    far = (me_y + 2) % ND
    for m in range(NM):
        wait(hid.at[pl.ds(0, ND - 1), m], y_r.at[0, m])
        wait(nsl.at[:, m], y_r.at[1, m])
        wait(gsl.at[:, m], y_r.at[2, m])
        for s in range(2):
            wait(dgu.at[y_down, m, s], yd_r.at[1 - s, m, s])
            wait(dgu.at[far, m, s], yf_r.at[m, s])
    rows = ND * NM * 2 * R
    n_t = nsl[...].reshape(rows, DS)
    gg_ref[...] = dot(n_t, dgu[:, :, :, 0].reshape(rows, F), TN).astype(BF)
    ug_ref[...] = dot(n_t, dgu[:, :, :, 1].reshape(rows, F), TN).astype(BF)
    dg_ref[...] = dot(hid[...].reshape(rows, F), gsl[...].reshape(rows, DS), TN).astype(BF)

    wait(zbuf, r2_r)
    total = zbuf[0]
    for k in range(1, NZ):
        total = total + zbuf[k]
    rg_ref[...] = total

    for kind, out in enumerate((act_ref, igr_ref)):
        for m in range(NM):
            wait(actb.at[kind, oc, m, c], ac_r.at[kind, m])
            for half in range(2):
                v = actb[kind, half, m, c].astype(F32)
                out[m, :, half * H:half * H + Q] = v[:8].astype(BF)
                out[m, :, half * H + Q:(half + 1) * H] = v[8:].astype(BF)

    for kind in range(2):
        wait(ebs.at[kind], e_s.at[kind])
        p, r = ((ps_f, rf), (ps_b, rb))[kind]
        sends = me_l < NP - 1 if kind == 0 else me_l > 0
        origin = me_l == 0 if kind == 0 else last == 1
        for m in range(NM):
            wait(actb.at[kind, 0, m, 0], ac_s.at[kind, m])
            for s in range(2):
                wait(xall.at[kind, m, s, 0], fw_s.at[kind, m, s])
                wait(p.at[m, s], pr_s.at[kind, m, s])
                wait(r.at[m, s, pl.ds(0, NZ - 1)], rs_s.at[kind, m, s])

                @pl.when(sends)
                def _():
                    wait(xall.at[kind, m, s, 0], ag_s.at[kind, m, s])

                @pl.when(origin)
                def _():
                    wait(xall.at[kind, m, s, 0, pl.ds(0, 16 * NZ - 16)], ag0_s.at[kind, m, s])

    wait(pmall.at[pl.ds(0, NE - 1)], m_s)
    for m in range(NM):
        for i, ref in enumerate((hid, nsl, gsl)):
            wait(ref.at[pl.ds(0, ND - 1), m], y_s.at[i, m])
        for s in range(2):
            wait(dgu.at[0, m, s], yd_s.at[0, m, s])
            wait(dgu.at[0, m, s], yd_s.at[1, m, s])
            wait(dgu.at[0, m, s], yf_s.at[m, s])
    for j in range(ND // 2):
        @pl.when(c * (ND // 2) + j != me_y)
        def _():
            wait(ybuf.at[0], r1_s.at[j])

    @pl.when(mine)
    def _():
        wait(zbuf, r2_s)
        wait(zbuf.at[pl.ds(0, NZ - 1)], r2_s)


def local(embedded, out_grad, norm_gain, router_weight, gate_weight, up_weight, down_weight, routing):
    NM, _, D = embedded.shape
    F = gate_weight.shape[-1]
    NE, ND, NP = lax.axis_size("expert"), lax.axis_size("dp"), lax.axis_size("pipe")
    NZ, H, Q, R, DS = NE // 2, D // 2, D // 4, NE * 4, D // ND
    QX = Q + 128
    V = pl.BlockSpec(memory_space=pltpu.VMEM)
    A = pl.BlockSpec(memory_space=pl.ANY)

    def vm(*shape):
        return pltpu.VMEM(shape, BF)

    def vf(*shape):
        return pltpu.VMEM(shape, F32)

    sem = pltpu.SemaphoreType.DMA
    unit = sem((2, NM, 2))
    shape = jax.ShapeDtypeStruct
    act, igr, gg, ug, dg, rg = pl.pallas_call(
        functools.partial(kernel, (NM, D, F, NE, ND, NP)),
        name="moe_layers",
        in_specs=[V, V, V, V, V, A, A, A],
        out_specs=[V] * 6,
        out_shape=[
            shape((NM, 8, D), BF), shape((NM, 8, D), BF), shape((DS, F), BF), shape((DS, F), BF),
            shape((F, DS), BF), shape((NE + 8, 128), F32),
        ],
        scratch_shapes=[
            vm(D, F), vm(D, F), vm(F, D),
            vm(2, NM, 16, Q), vm(2, 2, NM, 16, Q),
            vf(NE, NM, 8, 128),
            vm(2, NM, 2, 2, NZ * 16, Q), vm(NM, 2, R, D), vm(NM, 2, R, D),
            vf(NM, 2, R, F), vf(NM, 2, R, F), vm(NM, 2, R, F),
            vf(NM, 2, R, 128), vf(NM, 2, R, 128), vf(NM, 2, R, NE),
            vm(NM, 2, R, H), vm(NM, 2, R, H), vm(NM, 2, R, H + 128), vm(NM, 2, R, H + 128),
            vf(NM, 2, R, H), vf(R, H + 128), vm(NM, 2, NZ * 16, Q), vm(NM, 2, NZ * 16, QX),
            vm(NM, 2, NZ, 16, Q), vm(NM, 2, NZ, 16, QX), vm(2, 2, NM, 2, 16, Q),
            vm(ND, NM, 2, R, DS), vm(ND, NM, 2, R, DS), vm(ND, NM, 2, R, F), vm(ND, NM, 2, 2, R, F),
            vf(NE + 8, H), vf(NE + 8, H), vf(ND, NE + 8, DS), vf(NE + 8, DS), vf(NZ, NE + 8, 128),
            sem((3,)), sem((2,)), sem((2,)), sem, sem,
            unit, unit, unit, unit, unit, unit, unit, unit, unit, sem((2, NM)), sem((2, NM)),
            sem((3, NM)), sem((3, NM)), unit, unit, sem((NM, 2)), sem((NM, 2)),
            sem((ND // 2,)), sem, sem, sem,
        ],
        compiler_params=pltpu.CompilerParams(
            collective_id=0, has_side_effects=True, vmem_limit_bytes=58 * 2**20
        ),
    )(
        embedded, out_grad, routing[0], norm_gain, router_weight[0].T,
        gate_weight[0, 0], up_weight[0, 0], down_weight[0, 0],
    )
    per = DS // NE
    part = lax.dynamic_slice_in_dim(rg, lax.axis_index("expert") * per % 128, per, 1)
    return (
        act[None], igr[None], gg[None, None], ug[None, None], dg[None, None],
        part[:NE].T[None], part[NE][None],
    )


def solution(mesh):
    return jax.shard_map(
        local,
        mesh=mesh,
        in_specs=(
            P(None, ("dp", "expert"), None),
            P(None, ("dp", "expert"), None),
            P("pipe", None),
            P("pipe", None, None),
            P("pipe", "expert", None, None),
            P("pipe", "expert", None, None),
            P("pipe", "expert", None, None),
            P("pipe", None, ("dp", "expert"), None),
        ),
        out_specs=(
            P("pipe", None, ("dp", "expert"), None),
            P("pipe", None, ("dp", "expert"), None),
            P("pipe", "expert", "dp", None),
            P("pipe", "expert", "dp", None),
            P("pipe", "expert", None, "dp"),
            P("pipe", ("dp", "expert"), None),
            P("pipe", ("dp", "expert")),
        ),
        check_vma=False,
    )
```

```python
import functools

import jax
import jax.numpy as jnp
from jax import lax
from jax.experimental import pallas as pl
from jax.experimental.pallas import tpu as pltpu
from jax.sharding import PartitionSpec as P

EPSILON = 1e-06
MESH = pl.DeviceIdType.MESH
BF = jnp.bfloat16
F32 = jnp.float32
NN = (((1,), (0,)), ((), ()))
NT = (((1,), (1,)), ((), ()))
TN = (((0,), (0,)), ((), ()))


def dot(a, b, dims):
    return lax.dot_general(a, b, dims, preferred_element_type=F32)


def col(value):
    return jnp.sum(value, axis=-1, keepdims=True)


def fold(value):
    half = value.shape[1] // 2
    return jnp.concatenate([value[:, :half], value[:, half:]], axis=0)


def twice(value):
    return jnp.concatenate([value, value], axis=0)


def hand_over(*refs):
    sems = refs[21]
    count = range(7)
    come = [pltpu.make_async_copy(refs[i], refs[14 + i], sems.at[0, i]) for i in count]
    go = [pltpu.make_async_copy(refs[14 + i], refs[7 + i], sems.at[1, i]) for i in count]
    for move in come:
        move.start()
    for i in count:
        come[i].wait()
        go[i].start()
    for move in go:
        move.wait()


def kernel(
    sizes,
    emb_ref, og_ref, ids_ref, gain_ref, rw_ref, gate_hbm, up_hbm, down_hbm,
    act_ref, igr_ref, gg_ref, ug_ref, dg_ref, rt_ref, gn_ref,
    wg, wu, wd, wgt, wut, wdt, ebs, src0, pmall, xall, nrm, gfull, gpre, upre, hidb, invs, wst, lgs,
    ps_f, pr_f, ps_b, pr_b, qo_f, qo_b, qf, qb, rf, rb, actb,
    nsl, gsl, hid, dgu, racc, rgs, ybuf, ysum, zbuf,
    w_sem, e_s, e_r, m_s, m_r, ag0_s, ag_s, ag_r, fw_s, fw_r, pr_s, pr_rs, rs_s, rs_r, ac_s, ac_r,
    y_s, y_r, yd_s, yd_r, yf_s, yf_r, r1_s, r1_r, r2_s, r2_r,
):
    NM, D, F, NE, ND, NP = sizes
    NZ, H, Q, R, DS = NE // 2, D // 2, D // 4, NE * 4, D // ND
    QX = Q + 128
    me_y = lax.axis_index("dp")
    me_l = lax.axis_index("pipe")
    me_e = lax.axis_index("expert")
    z = me_e // 2
    c = me_e % 2
    oc = 1 - c
    partner = {"expert": me_e + 1 - 2 * c}
    own_rows = pl.ds(pl.multiple_of(z * 16, 16), 16)
    own_tokens = pl.ds(pl.multiple_of(z * 8, 8), 8)
    own_half = pl.ds(pl.multiple_of(c * H, H), H)
    other_half = pl.ds(pl.multiple_of(oc * H, H), H)
    last = (me_l + 1) // NP
    far_first = sorted(range(1, NZ), key=lambda k: (-min(k, NZ - k), k))
    y_up, y_down = (me_y + 1) % ND, (me_y + ND - 1) % ND

    def send(src, dst, ss, rs, dev):
        pltpu.make_async_remote_copy(
            src_ref=src, dst_ref=dst, send_sem=ss, recv_sem=rs, device_id=dev, device_id_type=MESH
        ).start()

    def copy(src, dst, sem):
        pltpu.make_async_copy(src, dst, sem).start()

    def wait(ref, sem):
        pltpu.make_async_copy(ref, ref, sem).wait()

    copy(gate_hbm, wg, w_sem.at[0])
    copy(up_hbm, wu, w_sem.at[1])
    copy(down_hbm, wd, w_sem.at[2])

    barrier = pltpu.get_barrier_semaphore()

    def hello(dev):
        pl.semaphore_signal(barrier, inc=1, device_id=dev, device_id_type=MESH)

    hello(partner)
    for k in range(1, NZ):
        for cc in range(2):
            hello({"expert": 2 * ((z + k) % NZ) + cc})
    for j in range(1, ND):
        hello({"dp": (me_y + j) % ND})
    for step in (1, NP - 1):
        for k in range(NZ):
            hello({"pipe": (me_l + step) % NP, "expert": 2 * ((z + k) % NZ) + c})

    mine0 = (c == 0).astype(F32)
    for kind, ref in enumerate((emb_ref, og_ref)):
        for m in range(NM):
            v = ref[m].astype(F32)
            low, high = v[:, :H], v[:, H:]
            src0[kind, c, m] = fold(low * mine0 + high * (1.0 - mine0)).astype(BF)
            ebs[kind, m] = fold(high * mine0 + low * (1.0 - mine0)).astype(BF)
    lanes8 = lax.broadcasted_iota(jnp.int32, (8, 128), 1)
    for m in range(NM):
        ids = ids_ref[m]
        table = jnp.zeros((8, 128), F32)
        for k in range(ids.shape[1]):
            table = table + (ids[:, k:k + 1] == lanes8).astype(F32)
        pmall[c * NZ + z, m] = table
    racc[...] = jnp.zeros(racc.shape, F32)

    pl.semaphore_wait(barrier, 1 + 2 * (NZ - 1) + (ND - 1) + 2 * NZ)

    for kind in range(2):
        send(ebs.at[kind], src0.at[kind, c], e_s.at[kind], e_r.at[kind], partner)
    my_table = pmall.at[c * NZ + z]
    send(my_table, my_table, m_s, m_r, partner)
    for k in range(1, NZ):
        for cc in range(2):
            send(my_table, my_table, m_s, m_r, {"expert": 2 * ((z + k) % NZ) + cc})

    def gather(kind, m, s, src, sems, section):
        for k in far_first + [0]:
            send(
                src, xall.at[kind, m, s, c, own_rows], sems.at[kind, m, s], ag_r.at[kind, m, s],
                {"pipe": section, "expert": 2 * ((z + k) % NZ) + c},
            )

    for kind in range(2):
        wait(src0.at[kind, oc], e_r.at[kind])

        @pl.when(me_l == NP - 1 - kind)
        def _():
            for m in range(NM):
                for s in range(2):
                    gather(kind, m, s, src0.at[kind, s, m], ag0_s, (NP - 1) * kind)

    wait(pmall.at[pl.ds(0, NE - 1)], m_r)
    wait(wg, w_sem.at[0])
    wait(wu, w_sem.at[1])
    wait(wd, w_sem.at[2])
    for j in range(D // 256):
        rows = slice(256 * j, 256 * j + 256)
        wgt[:, rows] = wg[rows, :].T
        wut[:, rows] = wu[rows, :].T
        wdt[rows, :] = wd[:, rows].T

    def arrive(kind, m, s):
        got = xall.at[kind, m, s, c]
        wait(got, ag_r.at[kind, m, s])
        send(got, got, fw_s.at[kind, m, s], fw_r.at[kind, m, s], partner)
        wait(xall.at[kind, m, s, oc], fw_r.at[kind, m, s])

    @pl.when(last == 1)
    def _():
        for m in range(NM):
            for s in range(2):
                arrive(1, m, s)

    def quarters(kind, m, s):
        out = []
        for half in range(2):
            v = xall[kind, m, s, half].astype(F32).reshape(NZ, 2, 8, Q)
            out += [v[:, 0].reshape(R, Q), v[:, 1].reshape(R, Q)]
        return out

    lane_e = lax.broadcasted_iota(jnp.int32, (R, NE), 1)
    lane_x = lax.broadcasted_iota(jnp.int32, (R, 128), 1)

    def forward_compute(m, s):
        xs = quarters(0, m, s)
        square = xs[0] * xs[0]
        for v in xs[1:]:
            square = square + v * v
        inv = lax.rsqrt(col(square) * (1.0 / D) + EPSILON)
        for i, v in enumerate(xs):
            nrm[m, s, :, i * Q:(i + 1) * Q] = (v * inv * gain_ref[0:1, i * Q:(i + 1) * Q]).astype(BF)
        normed = nrm[m, s]
        logits = dot(normed, rw_ref[...], NT)
        named = pmall[pl.ds(s * NZ, NZ), m].reshape(R, 128)[:, :NE]
        chosen = named * jax.nn.sigmoid(logits)
        w = col(jnp.where(lane_e == me_e, chosen, 0.0)) / col(chosen)
        invs[m, s] = jnp.broadcast_to(inv, (R, 128))
        wst[m, s] = jnp.broadcast_to(w, (R, 128))
        lgs[m, s] = logits
        a = dot(normed, wg[...], NN)
        b = dot(normed, wu[...], NN)
        gpre[m, s] = a
        upre[m, s] = b
        h = (a * jax.nn.sigmoid(a) * b).astype(BF)
        hidb[m, s] = h
        hid[me_y, m, s] = (h.astype(F32) * w).astype(BF)
        ps_f[m, s] = (dot(h, wd[:, other_half], NN) * w).astype(BF)
        send(ps_f.at[m, s], pr_f.at[m, s], pr_s.at[0, m, s], pr_rs.at[0, m, s], partner)
        qo_f[m, s] = dot(h, wd[:, own_half], NN) * w

    def scatter(kind, m, s, q, r):
        for k in far_first:
            zz = (z + k) % NZ
            send(
                q.at[m, s, pl.ds(pl.multiple_of(zz * 16, 16), 16)], r.at[m, s, z],
                rs_s.at[kind, m, s], rs_r.at[kind, m, s], {"expert": 2 * zz + c},
            )
        copy(q.at[m, s, own_rows], r.at[m, s, z], rs_r.at[kind, m, s])

    def part(ref, yy):
        return ref.at[:, pl.ds(pl.multiple_of(yy * DS, DS), DS)]

    def folded(v):
        width = v.shape[1] // 2
        low, high = v[:, :width].reshape(NZ, 1, 8, width), v[:, width:].reshape(NZ, 1, 8, width)
        return jnp.concatenate([low, high], axis=1).reshape(NZ * 16, width)

    def forward_scatter(m, s):
        wait(pr_f.at[m, s], pr_rs.at[0, m, s])
        qf[m, s] = folded(qo_f[m, s] + pr_f[m, s].astype(F32)).astype(BF)
        scatter(0, m, s, qf, rf)

    def forward_replicas(m, s):
        for j in range(1, ND):
            yy = (me_y + j) % ND
            mine = hid.at[me_y, m, s]
            send(mine, mine, y_s.at[0, m], y_r.at[0, m], {"dp": yy})
            send(part(nrm.at[m, s], yy), nsl.at[me_y, m, s], y_s.at[1, m], y_r.at[1, m], {"dp": yy})
        copy(part(nrm.at[m, s], me_y), nsl.at[me_y, m, s], y_r.at[1, m])

    def keep(kind, m, s):
        block = actb.at[kind, c, m, s]

        @pl.when(oc == s)
        def _():
            send(block, block, ac_s.at[kind, m], ac_r.at[kind, m], partner)

    def forward_result(m, s):
        wait(rf.at[m, s], rs_r.at[0, m, s])
        total = xall[0, m, s, c, own_rows].astype(F32)
        for k in range(NZ):
            total = total + rf[m, s, k].astype(F32)
        actb[0, c, m, s] = total.astype(BF)

        @pl.when(last == 0)
        def _():
            gather(0, m, s, actb.at[0, c, m, s], ag_s, me_l + 1)

        keep(0, m, s)

    def backward_compute(m, s):
        for i, v in enumerate(quarters(1, m, s)):
            gfull[m, s, :, i * Q:(i + 1) * Q] = v.astype(BF)
        dh = dot(gfull[m, s], wdt[...], NN)
        w = wst[m, s][:, :1]
        a = gpre[m, s]
        b = upre[m, s]
        dw = col(dh * hidb[m, s].astype(F32))
        dhw = dh * w
        sg = jax.nn.sigmoid(a)
        dgate = (dhw * b * sg * (1.0 + a * (1.0 - sg))).astype(BF)
        dupv = (dhw * (a * sg)).astype(BF)
        dgu[me_y, m, s, 0] = dgate
        dgu[me_y, m, s, 1] = dupv
        sv = col(dgate.astype(F32) * a + dupv.astype(F32) * b)
        dw_hi = dw.astype(BF).astype(F32)
        sv_hi = sv.astype(BF).astype(F32)
        ext = jnp.where(lane_x == me_e, dw_hi, 0.0)
        ext = jnp.where(lane_x == NE + me_e, dw - dw_hi, ext)
        ext = jnp.where(lane_x == 2 * NE + me_e, sv_hi, ext)
        ext = jnp.where(lane_x == 3 * NE + me_e, sv - sv_hi, ext)
        ps_b[m, s, :, :H] = (
            dot(dgate, wgt[:, other_half], NN) + dot(dupv, wut[:, other_half], NN)
        ).astype(BF)
        ps_b[m, s, :, H:] = ext.astype(BF)
        send(ps_b.at[m, s], pr_b.at[m, s], pr_s.at[1, m, s], pr_rs.at[1, m, s], partner)
        qo_b[:, :H] = dot(dgate, wgt[:, own_half], NN) + dot(dupv, wut[:, own_half], NN)
        qo_b[:, H:] = ext

    def backward_scatter(m, s):
        wait(pr_b.at[m, s], pr_rs.at[1, m, s])
        q = qo_b[...] + pr_b[m, s].astype(F32)
        qb[m, s, :, :Q] = folded(q[:, :H]).astype(BF)
        ext = q[:, H:].reshape(NZ, 1, 8, 128)
        qb[m, s, :, Q:] = (
            jnp.concatenate([ext, jnp.zeros_like(ext)], axis=1).reshape(NZ * 16, 128).astype(BF)
        )
        scatter(1, m, s, qb, rb)

    def backward_replicas(m, s):
        mine = dgu.at[me_y, m, s]
        send(mine, mine, yd_s.at[0, m, s], yd_r.at[0, m, s], {"dp": y_up})
        send(mine, mine, yd_s.at[1, m, s], yd_r.at[1, m, s], {"dp": y_down})
        for j in range(1, ND):
            yy = (me_y + j) % ND
            send(part(gfull.at[m, s], yy), gsl.at[me_y, m, s], y_s.at[2, m], y_r.at[2, m], {"dp": yy})
        copy(part(gfull.at[m, s], me_y), gsl.at[me_y, m, s], y_r.at[2, m])

    def pass_on(m):
        for s, source, target in ((0, y_down, y_up), (1, y_up, y_down)):
            block = dgu.at[source, m, s]
            wait(block, yd_r.at[s, m, s])
            send(block, block, yf_s.at[m, s], yf_r.at[m, s], {"dp": target})

    def backward_result(m, s):
        wait(rb.at[m, s], rs_r.at[1, m, s])
        total = rb[m, s, 0].astype(F32)
        for k in range(1, NZ):
            total = total + rb[m, s, k].astype(F32)
        ext = total[:8, Q:]
        dw = ext[:, :NE] + ext[:, NE:2 * NE]
        sv = col(ext[:, 2 * NE:3 * NE] + ext[:, 3 * NE:4 * NE])
        logits = lgs[m, s, own_tokens]
        named = pmall[s * NZ + z, m][:, :NE]
        chosen = named * jax.nn.sigmoid(logits)
        prob_total = col(chosen)
        weights = chosen / prob_total
        dchosen = (dw - col(dw * weights)) / prob_total
        dlogits = dchosen * chosen * (1.0 - chosen)
        dl_hi = dlogits.astype(BF).astype(F32)
        dl = jnp.concatenate([dl_hi, dlogits - dl_hi], axis=0).astype(BF)
        term = dot(dl, rw_ref[:, own_half], NN)
        dnormed = total[:, :Q] + fold(term[:8] + term[8:])
        inv = twice(invs[m, s, own_tokens][:, :1])
        gain_row = gain_ref[0:1, own_half]
        gain = jnp.concatenate(
            [jnp.broadcast_to(gain_row[:, :Q], (8, Q)), jnp.broadcast_to(gain_row[:, Q:], (8, Q))],
            axis=0,
        )
        x = xall[0, m, s, c, own_rows].astype(F32)
        g = xall[1, m, s, c, own_rows].astype(F32)
        along = twice((sv + col(dlogits * logits)) * (1.0 / D))
        dinput = inv * (dnormed * gain - x * (inv * along))
        actb[1, c, m, s] = (g + dinput).astype(BF)

        @pl.when(me_l > 0)
        def _():
            gather(1, m, s, actb.at[1, c, m, s], ag_s, me_l - 1)

        keep(1, m, s)
        normed = x * inv * gain
        gained = dnormed * x * inv
        for i in range(2):
            rows = slice(8 * i, 8 * i + 8)
            cols = slice(Q * i, Q * i + Q)
            racc[0:NE, cols] = racc[0:NE, cols] + dot(dl, twice(normed[rows]).astype(BF), TN)
            racc[NE:NE + 8, cols] = racc[NE:NE + 8, cols] + gained[rows]

    units = 2 * NM

    def step(k, carry):
        u = k % units
        m, s = u // 2, u % 2
        before = (u + units - 1) % units
        bm, bs = before // 2, before % 2
        first = k < units
        is_last = last == 1
        forward = (first & (last == 0)) | ((k >= units) & is_last)
        backward = ((k >= units) & (last == 0)) | (first & is_last)

        @pl.when(first)
        def _():
            arrive(0, m, s)
            forward_compute(m, s)

        @pl.when(backward & (last == 0))
        def _():
            arrive(1, m, s)

        @pl.when(backward)
        def _():
            backward_compute(m, s)

        @pl.when(forward & (u > 0))
        def _():
            forward_result(bm, bs)

        @pl.when(backward & (u > 0))
        def _():
            backward_result(bm, bs)

        @pl.when(forward)
        def _():
            forward_scatter(m, s)
            forward_replicas(m, s)

        @pl.when(backward)
        def _():
            backward_scatter(m, s)
            backward_replicas(m, s)

        @pl.when(backward & (s == 1) & (m > 0))
        def _():
            pass_on(m - 1)

        @pl.when(forward & (u == units - 1))
        def _():
            forward_result(m, s)

        @pl.when(backward & (u == units - 1))
        def _():
            backward_result(m, s)

        return carry

    lax.fori_loop(0, 2 * units, step, 0)
    pass_on(NM - 1)

    rgs[0:NE] = racc[0:NE]
    rgs[NE:NE + 8] = jnp.broadcast_to(
        jnp.sum(racc[NE:NE + 8], axis=0, keepdims=True), (8, H)
    )
    mine = c == me_y // (ND // 2)
    for j in range(ND // 2):
        yy = c * (ND // 2) + j
        src = rgs.at[:, pl.ds(j * DS, DS)]

        @pl.when(yy != me_y)
        def _():
            send(src, ybuf.at[me_y], r1_s.at[j], r1_r, {"dp": yy})

        @pl.when(yy == me_y)
        def _():
            copy(src, ybuf.at[me_y], r1_r)

    far = (me_y + 2) % ND
    rows = ND * NM * 2 * R
    for m in range(NM):
        wait(hid.at[pl.ds(0, ND - 1), m], y_r.at[0, m])
        wait(nsl.at[:, m], y_r.at[1, m])
        wait(gsl.at[:, m], y_r.at[2, m])
    dg_ref[...] = dot(hid[...].reshape(rows, F), gsl[...].reshape(rows, DS), TN).astype(BF)

    per = DS // NE

    @pl.when(mine)
    def _():
        wait(ybuf, r1_r)
        total = ybuf[0]
        for j in range(1, ND):
            total = total + ybuf[j]
        ysum[...] = total
        for k in range(NZ):
            for cc in range(2):
                ee = 2 * ((z + k) % NZ) + (c + cc) % 2
                src = ysum.at[:, pl.ds(pl.multiple_of(ee * per // 128 * 128, 128), 128)]
                if k == 0 and cc == 0:
                    copy(src, zbuf.at[z], r2_r)
                else:
                    send(src, zbuf.at[z], r2_s, r2_r, {"expert": ee})

    for m in range(NM):
        for s in range(2):
            wait(dgu.at[y_down, m, s], yd_r.at[1 - s, m, s])
            wait(dgu.at[far, m, s], yf_r.at[m, s])
    n_t = nsl[...].reshape(rows, DS)
    gg_ref[...] = dot(n_t, dgu[:, :, :, 0].reshape(rows, F), TN).astype(BF)
    ug_ref[...] = dot(n_t, dgu[:, :, :, 1].reshape(rows, F), TN).astype(BF)

    wait(zbuf, r2_r)
    total = zbuf[0]
    for k in range(1, NZ):
        total = total + zbuf[k]
    picked = jnp.zeros((NE + 8, per), F32)
    for i in range(128 // per):
        picked = jnp.where(
            lax.rem(me_e, 128 // per) == i, total[:, i * per:(i + 1) * per], picked
        )
    rt_ref[...] = picked[:NE]
    gn_ref[...] = picked[NE:NE + 1]

    for kind, out in enumerate((act_ref, igr_ref)):
        for m in range(NM):
            wait(actb.at[kind, oc, m, c], ac_r.at[kind, m])
            for half in range(2):
                v = actb[kind, half, m, c].astype(F32)
                out[m, :, half * H:half * H + Q] = v[:8].astype(BF)
                out[m, :, half * H + Q:(half + 1) * H] = v[8:].astype(BF)

    for kind in range(2):
        wait(ebs.at[kind], e_s.at[kind])
        p, r = ((ps_f, rf), (ps_b, rb))[kind]
        sends = me_l < NP - 1 if kind == 0 else me_l > 0
        origin = me_l == NP - 1 - kind
        for m in range(NM):
            wait(actb.at[kind, 0, m, 0], ac_s.at[kind, m])
            for s in range(2):
                wait(xall.at[kind, m, s, 0], fw_s.at[kind, m, s])
                wait(p.at[m, s], pr_s.at[kind, m, s])
                wait(r.at[m, s, pl.ds(0, NZ - 1)], rs_s.at[kind, m, s])

                @pl.when(sends)
                def _():
                    wait(xall.at[kind, m, s, 0], ag_s.at[kind, m, s])

                @pl.when(origin)
                def _():
                    wait(xall.at[kind, m, s, 0], ag0_s.at[kind, m, s])

    wait(pmall.at[pl.ds(0, NE - 1)], m_s)
    for m in range(NM):
        for i, ref in enumerate((hid, nsl, gsl)):
            wait(ref.at[pl.ds(0, ND - 1), m], y_s.at[i, m])
        for s in range(2):
            wait(dgu.at[0, m, s], yd_s.at[0, m, s])
            wait(dgu.at[0, m, s], yd_s.at[1, m, s])
            wait(dgu.at[0, m, s], yf_s.at[m, s])
    for j in range(ND // 2):
        @pl.when(c * (ND // 2) + j != me_y)
        def _():
            wait(ybuf.at[0], r1_s.at[j])

    @pl.when(mine)
    def _():
        wait(zbuf, r2_s)
        wait(zbuf.at[pl.ds(0, NZ - 1)], r2_s)


def local(embedded, out_grad, norm_gain, router_weight, gate_weight, up_weight, down_weight, routing):
    NM, _, D = embedded.shape
    F = gate_weight.shape[-1]
    NE, ND, NP = lax.axis_size("expert"), lax.axis_size("dp"), lax.axis_size("pipe")
    NZ, H, Q, R, DS = NE // 2, D // 2, D // 4, NE * 4, D // ND
    QX = Q + 128
    V = pl.BlockSpec(memory_space=pltpu.VMEM)
    A = pl.BlockSpec(memory_space=pl.ANY)

    def vm(*shape):
        return pltpu.VMEM(shape, BF)

    def vf(*shape):
        return pltpu.VMEM(shape, F32)

    sem = pltpu.SemaphoreType.DMA
    unit = sem((2, NM, 2))
    shape = jax.ShapeDtypeStruct
    per = DS // NE
    results = pl.pallas_call(
        functools.partial(kernel, (NM, D, F, NE, ND, NP)),
        name="moe_layers",
        in_specs=[V, V, V, V, V, A, A, A],
        out_specs=[V] * 7,
        out_shape=[
            shape((NM, 8, D), BF), shape((NM, 8, D), BF), shape((DS, F), BF), shape((DS, F), BF),
            shape((F, DS), BF), shape((NE, per), F32), shape((1, per), F32),
        ],
        scratch_shapes=[
            vm(D, F), vm(D, F), vm(F, D), vm(F, D), vm(F, D), vm(D, F),
            vm(2, NM, 16, Q), vm(2, 2, NM, 16, Q),
            vf(NE, NM, 8, 128),
            vm(2, NM, 2, 2, NZ * 16, Q), vm(NM, 2, R, D), vm(NM, 2, R, D),
            vf(NM, 2, R, F), vf(NM, 2, R, F), vm(NM, 2, R, F),
            vf(NM, 2, R, 128), vf(NM, 2, R, 128), vf(NM, 2, R, NE),
            vm(NM, 2, R, H), vm(NM, 2, R, H), vm(NM, 2, R, H + 128), vm(NM, 2, R, H + 128),
            vf(NM, 2, R, H), vf(R, H + 128), vm(NM, 2, NZ * 16, Q), vm(NM, 2, NZ * 16, QX),
            vm(NM, 2, NZ, 16, Q), vm(NM, 2, NZ, 16, QX), vm(2, 2, NM, 2, 16, Q),
            vm(ND, NM, 2, R, DS), vm(ND, NM, 2, R, DS), vm(ND, NM, 2, R, F), vm(ND, NM, 2, 2, R, F),
            vf(NE + 8, H), vf(NE + 8, H), vf(ND, NE + 8, DS), vf(NE + 8, DS), vf(NZ, NE + 8, 128),
            sem((3,)), sem((2,)), sem((2,)), sem, sem,
            unit, unit, unit, unit, unit, unit, unit, unit, unit, sem((2, NM)), sem((2, NM)),
            sem((3, NM)), sem((3, NM)), unit, unit, sem((NM, 2)), sem((NM, 2)),
            sem((ND // 2,)), sem, sem, sem,
        ],
        compiler_params=pltpu.CompilerParams(
            collective_id=0, has_side_effects=True, vmem_limit_bytes=58 * 2**20
        ),
    )(
        embedded, out_grad, routing[0], norm_gain, router_weight[0].T,
        gate_weight[0, 0], up_weight[0, 0], down_weight[0, 0],
    )
    act, igr, gg, ug, dg, rt, gn = pl.pallas_call(
        hand_over,
        name="hand_over",
        in_specs=[A] * 7,
        out_specs=[A] * 7,
        out_shape=[shape(v.shape, v.dtype) for v in results],
        scratch_shapes=[pltpu.VMEM(v.shape, v.dtype) for v in results] + [sem((2, 7))],
        compiler_params=pltpu.CompilerParams(vmem_limit_bytes=58 * 2**20),
    )(*results)
    return (
        act[None], igr[None], gg[None, None], ug[None, None], dg[None, None], rt.T[None], gn,
    )


def solution(mesh):
    return jax.shard_map(
        local,
        mesh=mesh,
        in_specs=(
            P(None, ("dp", "expert"), None),
            P(None, ("dp", "expert"), None),
            P("pipe", None),
            P("pipe", None, None),
            P("pipe", "expert", None, None),
            P("pipe", "expert", None, None),
            P("pipe", "expert", None, None),
            P("pipe", None, ("dp", "expert"), None),
        ),
        out_specs=(
            P("pipe", None, ("dp", "expert"), None),
            P("pipe", None, ("dp", "expert"), None),
            P("pipe", "expert", "dp", None),
            P("pipe", "expert", "dp", None),
            P("pipe", "expert", None, "dp"),
            P("pipe", ("dp", "expert"), None),
            P("pipe", ("dp", "expert")),
        ),
        check_vma=False,
    )
```

```python
import functools

import jax
import jax.numpy as jnp
from jax import lax
from jax.experimental import pallas as pl
from jax.experimental.pallas import tpu as pltpu
from jax.sharding import PartitionSpec as P

EPSILON = 1e-06
MESH = pl.DeviceIdType.MESH
BF = jnp.bfloat16
F32 = jnp.float32
NN = (((1,), (0,)), ((), ()))
NT = (((1,), (1,)), ((), ()))
TN = (((0,), (0,)), ((), ()))


def dot(a, b, dims):
    return lax.dot_general(a, b, dims, preferred_element_type=F32)


def col(value):
    return jnp.sum(value, axis=-1, keepdims=True)


def fold(value):
    half = value.shape[1] // 2
    return jnp.concatenate([value[:, :half], value[:, half:]], axis=0)


def twice(value):
    return jnp.concatenate([value, value], axis=0)


def hand_over(*refs):
    sems = refs[21]
    count = range(7)
    come = [pltpu.make_async_copy(refs[i], refs[14 + i], sems.at[0, i]) for i in count]
    go = [pltpu.make_async_copy(refs[14 + i], refs[7 + i], sems.at[1, i]) for i in count]
    for move in come:
        move.start()
    for i in count:
        come[i].wait()
        go[i].start()
    for move in go:
        move.wait()


def kernel(
    sizes,
    emb_ref, og_ref, ids_ref, gain_ref, rw_ref, gate_hbm, up_hbm, down_hbm,
    act_ref, igr_ref, gg_ref, ug_ref, dg_ref, rt_ref, gn_ref,
    wg, wu, wd, wgt, wut, wdt, ebs, src0, pmall, xall, nrm, gfull, gpre, upre, hidb, invs, wst, lgs,
    ps_f, pr_f, ps_b, pr_b, qo_f, qo_b, qf, qb, rf, rb, actb,
    nsl, gsl, hid, dgu, racc, rgs, ybuf, ysum, zbuf,
    w_sem, e_s, e_r, m_s, m_r, ag0_s, ag_s, ag_r, fw_s, fw_r, pr_s, pr_rs, rs_s, rs_r, ac_s, ac_r,
    y_s, y_r, yd_s, yd_r, yf_s, yf_r, yl_r, yp_s, yp_r, r1_s, r1_r, r2_s, r2_r,
):
    NM, D, F, NE, ND, NP = sizes
    NZ, H, Q, R, DS = NE // 2, D // 2, D // 4, NE * 4, D // ND
    QX = Q + 128
    me_y = lax.axis_index("dp")
    me_l = lax.axis_index("pipe")
    me_e = lax.axis_index("expert")
    z = me_e // 2
    c = me_e % 2
    oc = 1 - c
    partner = {"expert": me_e + 1 - 2 * c}
    own_rows = pl.ds(pl.multiple_of(z * 16, 16), 16)
    own_tokens = pl.ds(pl.multiple_of(z * 8, 8), 8)
    own_half = pl.ds(pl.multiple_of(c * H, H), H)
    other_half = pl.ds(pl.multiple_of(oc * H, H), H)
    last = (me_l + 1) // NP
    far_first = sorted(range(1, NZ), key=lambda k: (-min(k, NZ - k), k))
    y_up, y_down = (me_y + 1) % ND, (me_y + ND - 1) % ND

    def send(src, dst, ss, rs, dev):
        pltpu.make_async_remote_copy(
            src_ref=src, dst_ref=dst, send_sem=ss, recv_sem=rs, device_id=dev, device_id_type=MESH
        ).start()

    def copy(src, dst, sem):
        pltpu.make_async_copy(src, dst, sem).start()

    def wait(ref, sem):
        pltpu.make_async_copy(ref, ref, sem).wait()

    copy(gate_hbm, wg, w_sem.at[0])
    copy(up_hbm, wu, w_sem.at[1])
    copy(down_hbm, wd, w_sem.at[2])

    barrier = pltpu.get_barrier_semaphore()

    def hello(dev):
        pl.semaphore_signal(barrier, inc=1, device_id=dev, device_id_type=MESH)

    hello(partner)
    for k in range(1, NZ):
        for cc in range(2):
            hello({"expert": 2 * ((z + k) % NZ) + cc})
    for j in range(1, ND):
        hello({"dp": (me_y + j) % ND})
    for step in (1, NP - 1):
        for k in range(NZ):
            hello({"pipe": (me_l + step) % NP, "expert": 2 * ((z + k) % NZ) + c})

    mine0 = (c == 0).astype(F32)
    for kind, ref in enumerate((emb_ref, og_ref)):
        for m in range(NM):
            v = ref[m].astype(F32)
            low, high = v[:, :H], v[:, H:]
            src0[kind, c, m] = fold(low * mine0 + high * (1.0 - mine0)).astype(BF)
            ebs[kind, m] = fold(high * mine0 + low * (1.0 - mine0)).astype(BF)
    lanes8 = lax.broadcasted_iota(jnp.int32, (8, 128), 1)
    for m in range(NM):
        ids = ids_ref[m]
        table = jnp.zeros((8, 128), F32)
        for k in range(ids.shape[1]):
            table = table + (ids[:, k:k + 1] == lanes8).astype(F32)
        pmall[c * NZ + z, m] = table
    racc[...] = jnp.zeros(racc.shape, F32)

    pl.semaphore_wait(barrier, 1 + 2 * (NZ - 1) + (ND - 1) + 2 * NZ)

    for kind in range(2):
        send(ebs.at[kind], src0.at[kind, c], e_s.at[kind], e_r.at[kind], partner)
    my_table = pmall.at[c * NZ + z]
    send(my_table, my_table, m_s, m_r, partner)
    for k in range(1, NZ):
        for cc in range(2):
            send(my_table, my_table, m_s, m_r, {"expert": 2 * ((z + k) % NZ) + cc})

    def gather(kind, m, s, src, sems, section):
        for k in far_first + [0]:
            send(
                src, xall.at[kind, m, s, c, own_rows], sems.at[kind, m, s], ag_r.at[kind, m, s],
                {"pipe": section, "expert": 2 * ((z + k) % NZ) + c},
            )

    for kind in range(2):
        wait(src0.at[kind, oc], e_r.at[kind])

        @pl.when(me_l == NP - 1 - kind)
        def _():
            for m in range(NM):
                for s in range(2):
                    gather(kind, m, s, src0.at[kind, s, m], ag0_s, (NP - 1) * kind)

    wait(pmall.at[pl.ds(0, NE - 1)], m_r)
    wait(wg, w_sem.at[0])
    wait(wu, w_sem.at[1])
    wait(wd, w_sem.at[2])
    for j in range(D // 256):
        rows = slice(256 * j, 256 * j + 256)
        wgt[:, rows] = wg[rows, :].T
        wut[:, rows] = wu[rows, :].T
        wdt[rows, :] = wd[:, rows].T

    def arrive(kind, m, s):
        got = xall.at[kind, m, s, c]
        wait(got, ag_r.at[kind, m, s])
        send(got, got, fw_s.at[kind, m, s], fw_r.at[kind, m, s], partner)
        wait(xall.at[kind, m, s, oc], fw_r.at[kind, m, s])

    @pl.when(last == 1)
    def _():
        for m in range(NM):
            for s in range(2):
                arrive(1, m, s)

    def quarters(kind, m, s):
        out = []
        for half in range(2):
            v = xall[kind, m, s, half].astype(F32).reshape(NZ, 2, 8, Q)
            out += [v[:, 0].reshape(R, Q), v[:, 1].reshape(R, Q)]
        return out

    lane_e = lax.broadcasted_iota(jnp.int32, (R, NE), 1)
    lane_x = lax.broadcasted_iota(jnp.int32, (R, 128), 1)

    def forward_compute(m, s):
        xs = quarters(0, m, s)
        square = xs[0] * xs[0]
        for v in xs[1:]:
            square = square + v * v
        inv = lax.rsqrt(col(square) * (1.0 / D) + EPSILON)
        for i, v in enumerate(xs):
            nrm[m, s, :, i * Q:(i + 1) * Q] = (v * inv * gain_ref[0:1, i * Q:(i + 1) * Q]).astype(BF)
        normed = nrm[m, s]
        logits = dot(normed, rw_ref[...], NT)
        named = pmall[pl.ds(s * NZ, NZ), m].reshape(R, 128)[:, :NE]
        chosen = named * jax.nn.sigmoid(logits)
        w = col(jnp.where(lane_e == me_e, chosen, 0.0)) / col(chosen)
        invs[m, s] = jnp.broadcast_to(inv, (R, 128))
        wst[m, s] = jnp.broadcast_to(w, (R, 128))
        lgs[m, s] = logits
        a = dot(normed, wg[...], NN)
        b = dot(normed, wu[...], NN)
        gpre[m, s] = a
        upre[m, s] = b
        h = (a * jax.nn.sigmoid(a) * b).astype(BF)
        hidb[m, s] = h
        hid[me_y, m, s] = (h.astype(F32) * w).astype(BF)
        ps_f[m, s] = (dot(h, wd[:, other_half], NN) * w).astype(BF)
        send(ps_f.at[m, s], pr_f.at[m, s], pr_s.at[0, m, s], pr_rs.at[0, m, s], partner)
        qo_f[m, s] = dot(h, wd[:, own_half], NN) * w

    def scatter(kind, m, s, q, r):
        for k in far_first:
            zz = (z + k) % NZ
            send(
                q.at[m, s, pl.ds(pl.multiple_of(zz * 16, 16), 16)], r.at[m, s, z],
                rs_s.at[kind, m, s], rs_r.at[kind, m, s], {"expert": 2 * zz + c},
            )
        copy(q.at[m, s, own_rows], r.at[m, s, z], rs_r.at[kind, m, s])

    def part(ref, yy):
        return ref.at[:, pl.ds(pl.multiple_of(yy * DS, DS), DS)]

    def folded(v):
        width = v.shape[1] // 2
        low, high = v[:, :width].reshape(NZ, 1, 8, width), v[:, width:].reshape(NZ, 1, 8, width)
        return jnp.concatenate([low, high], axis=1).reshape(NZ * 16, width)

    def forward_scatter(m, s):
        wait(pr_f.at[m, s], pr_rs.at[0, m, s])
        qf[m, s] = folded(qo_f[m, s] + pr_f[m, s].astype(F32)).astype(BF)
        scatter(0, m, s, qf, rf)

    def forward_replicas(m, s):
        for j in range(1, ND):
            yy = (me_y + j) % ND
            mine = hid.at[me_y, m, s]
            send(mine, mine, y_s.at[0, m], y_r.at[0, m], {"dp": yy})
            send(part(nrm.at[m, s], yy), nsl.at[me_y, m, s], y_s.at[1, m], y_r.at[1, m], {"dp": yy})
        copy(part(nrm.at[m, s], me_y), nsl.at[me_y, m, s], y_r.at[1, m])

    def keep(kind, m, s):
        block = actb.at[kind, c, m, s]

        @pl.when(oc == s)
        def _():
            send(block, block, ac_s.at[kind, m], ac_r.at[kind, m], partner)

    def forward_result(m, s):
        wait(rf.at[m, s], rs_r.at[0, m, s])
        total = xall[0, m, s, c, own_rows].astype(F32)
        for k in range(NZ):
            total = total + rf[m, s, k].astype(F32)
        actb[0, c, m, s] = total.astype(BF)

        @pl.when(last == 0)
        def _():
            gather(0, m, s, actb.at[0, c, m, s], ag_s, me_l + 1)

        keep(0, m, s)

    def backward_compute(m, s):
        for i, v in enumerate(quarters(1, m, s)):
            gfull[m, s, :, i * Q:(i + 1) * Q] = v.astype(BF)
        dh = dot(gfull[m, s], wdt[...], NN)
        w = wst[m, s][:, :1]
        a = gpre[m, s]
        b = upre[m, s]
        dw = col(dh * hidb[m, s].astype(F32))
        dhw = dh * w
        sg = jax.nn.sigmoid(a)
        dgate = (dhw * b * sg * (1.0 + a * (1.0 - sg))).astype(BF)
        dupv = (dhw * (a * sg)).astype(BF)
        dgu[me_y, m, s, 0] = dgate
        dgu[me_y, m, s, 1] = dupv
        sv = col(dgate.astype(F32) * a + dupv.astype(F32) * b)
        dw_hi = dw.astype(BF).astype(F32)
        sv_hi = sv.astype(BF).astype(F32)
        ext = jnp.where(lane_x == me_e, dw_hi, 0.0)
        ext = jnp.where(lane_x == NE + me_e, dw - dw_hi, ext)
        ext = jnp.where(lane_x == 2 * NE + me_e, sv_hi, ext)
        ext = jnp.where(lane_x == 3 * NE + me_e, sv - sv_hi, ext)
        ps_b[m, s, :, :H] = (
            dot(dgate, wgt[:, other_half], NN) + dot(dupv, wut[:, other_half], NN)
        ).astype(BF)
        ps_b[m, s, :, H:] = ext.astype(BF)
        send(ps_b.at[m, s], pr_b.at[m, s], pr_s.at[1, m, s], pr_rs.at[1, m, s], partner)
        qo_b[:, :H] = dot(dgate, wgt[:, own_half], NN) + dot(dupv, wut[:, own_half], NN)
        qo_b[:, H:] = ext

    def backward_scatter(m, s):
        wait(pr_b.at[m, s], pr_rs.at[1, m, s])
        q = qo_b[...] + pr_b[m, s].astype(F32)
        qb[m, s, :, :Q] = folded(q[:, :H]).astype(BF)
        ext = q[:, H:].reshape(NZ, 1, 8, 128)
        qb[m, s, :, Q:] = (
            jnp.concatenate([ext, jnp.zeros_like(ext)], axis=1).reshape(NZ * 16, 128).astype(BF)
        )
        scatter(1, m, s, qb, rb)

    def backward_replicas(m, s):
        mine = dgu.at[me_y, m, s]
        send(mine, mine, yd_s.at[0, m, s], yd_r.at[0, m, s], {"dp": y_up})
        send(mine, mine, yd_s.at[1, m, s], yd_r.at[1, m, s], {"dp": y_down})
        copy(part(gfull.at[m, s], me_y), gsl.at[me_y, m, s], yl_r.at[m])

        @pl.when(s == c)
        def _():
            for j in range(1, ND):
                yy = (me_y + j) % ND
                send(
                    part(gfull.at[m, s], yy), gsl.at[me_y, m, s], y_s.at[2, m], y_r.at[2, m],
                    {"dp": yy},
                )

    def pass_on(m):
        for s, source, target in ((0, y_down, y_up), (1, y_up, y_down)):
            block = dgu.at[source, m, s]
            wait(block, yd_r.at[s, m, s])
            send(block, block, yf_s.at[m, s], yf_r.at[m, s], {"dp": target})
        wait(gsl.at[pl.ds(0, ND - 1), m, 0], y_r.at[2, m])
        for j in range(1, ND):
            block = gsl.at[(me_y + j) % ND, m, c]
            send(block, block, yp_s.at[m], yp_r.at[m], partner)

    def backward_result(m, s):
        wait(rb.at[m, s], rs_r.at[1, m, s])
        total = rb[m, s, 0].astype(F32)
        for k in range(1, NZ):
            total = total + rb[m, s, k].astype(F32)
        ext = total[:8, Q:]
        dw = ext[:, :NE] + ext[:, NE:2 * NE]
        sv = col(ext[:, 2 * NE:3 * NE] + ext[:, 3 * NE:4 * NE])
        logits = lgs[m, s, own_tokens]
        named = pmall[s * NZ + z, m][:, :NE]
        chosen = named * jax.nn.sigmoid(logits)
        prob_total = col(chosen)
        weights = chosen / prob_total
        dchosen = (dw - col(dw * weights)) / prob_total
        dlogits = dchosen * chosen * (1.0 - chosen)
        dl_hi = dlogits.astype(BF).astype(F32)
        dl = jnp.concatenate([dl_hi, dlogits - dl_hi], axis=0).astype(BF)
        term = dot(dl, rw_ref[:, own_half], NN)
        dnormed = total[:, :Q] + fold(term[:8] + term[8:])
        inv = twice(invs[m, s, own_tokens][:, :1])
        gain_row = gain_ref[0:1, own_half]
        gain = jnp.concatenate(
            [jnp.broadcast_to(gain_row[:, :Q], (8, Q)), jnp.broadcast_to(gain_row[:, Q:], (8, Q))],
            axis=0,
        )
        x = xall[0, m, s, c, own_rows].astype(F32)
        g = xall[1, m, s, c, own_rows].astype(F32)
        along = twice((sv + col(dlogits * logits)) * (1.0 / D))
        dinput = inv * (dnormed * gain - x * (inv * along))
        actb[1, c, m, s] = (g + dinput).astype(BF)

        @pl.when(me_l > 0)
        def _():
            gather(1, m, s, actb.at[1, c, m, s], ag_s, me_l - 1)

        keep(1, m, s)
        normed = x * inv * gain
        gained = dnormed * x * inv
        for i in range(2):
            rows = slice(8 * i, 8 * i + 8)
            cols = slice(Q * i, Q * i + Q)
            racc[0:NE, cols] = racc[0:NE, cols] + dot(dl, twice(normed[rows]).astype(BF), TN)
            racc[NE:NE + 8, cols] = racc[NE:NE + 8, cols] + gained[rows]

    units = 2 * NM

    def step(k, carry):
        u = k % units
        m, s = u // 2, u % 2
        before = (u + units - 1) % units
        bm, bs = before // 2, before % 2
        first = k < units
        is_last = last == 1
        forward = (first & (last == 0)) | ((k >= units) & is_last)
        backward = ((k >= units) & (last == 0)) | (first & is_last)

        @pl.when(first)
        def _():
            arrive(0, m, s)
            forward_compute(m, s)

        @pl.when(backward & (last == 0))
        def _():
            arrive(1, m, s)

        @pl.when(backward)
        def _():
            backward_compute(m, s)
            backward_replicas(m, s)

        @pl.when(forward)
        def _():
            forward_scatter(m, s)
            forward_replicas(m, s)

        @pl.when(backward)
        def _():
            backward_scatter(m, s)

        @pl.when(forward & (u > 0))
        def _():
            forward_result(bm, bs)

        @pl.when(backward & (u > 0))
        def _():
            backward_result(bm, bs)

        @pl.when(backward & (s == 1) & (m > 0))
        def _():
            pass_on(m - 1)

        @pl.when(forward & (u == units - 1))
        def _():
            forward_result(m, s)

        @pl.when(backward & (u == units - 1))
        def _():
            backward_result(m, s)

        return carry

    lax.fori_loop(0, 2 * units, step, 0)
    pass_on(NM - 1)

    rgs[0:NE] = racc[0:NE]
    rgs[NE:NE + 8] = jnp.broadcast_to(
        jnp.sum(racc[NE:NE + 8], axis=0, keepdims=True), (8, H)
    )
    mine = c == me_y // (ND // 2)
    for j in range(ND // 2):
        yy = c * (ND // 2) + j
        src = rgs.at[:, pl.ds(j * DS, DS)]

        @pl.when(yy != me_y)
        def _():
            send(src, ybuf.at[me_y], r1_s.at[j], r1_r, {"dp": yy})

        @pl.when(yy == me_y)
        def _():
            copy(src, ybuf.at[me_y], r1_r)

    far = (me_y + 2) % ND
    rows = ND * NM * 2 * R
    for m in range(NM):
        wait(hid.at[pl.ds(0, ND - 1), m], y_r.at[0, m])
        wait(nsl.at[:, m], y_r.at[1, m])
        wait(gsl.at[0, m], yl_r.at[m])
        wait(gsl.at[pl.ds(0, ND - 1), m, 0], yp_r.at[m])
    dg_ref[...] = dot(hid[...].reshape(rows, F), gsl[...].reshape(rows, DS), TN).astype(BF)

    per = DS // NE

    @pl.when(mine)
    def _():
        wait(ybuf, r1_r)
        total = ybuf[0]
        for j in range(1, ND):
            total = total + ybuf[j]
        ysum[...] = total
        for k in range(NZ):
            for cc in range(2):
                ee = 2 * ((z + k) % NZ) + (c + cc) % 2
                src = ysum.at[:, pl.ds(pl.multiple_of(ee * per // 128 * 128, 128), 128)]
                if k == 0 and cc == 0:
                    copy(src, zbuf.at[z], r2_r)
                else:
                    send(src, zbuf.at[z], r2_s, r2_r, {"expert": ee})

    for m in range(NM):
        for s in range(2):
            wait(dgu.at[y_down, m, s], yd_r.at[1 - s, m, s])
            wait(dgu.at[far, m, s], yf_r.at[m, s])
    n_t = nsl[...].reshape(rows, DS)
    gg_ref[...] = dot(n_t, dgu[:, :, :, 0].reshape(rows, F), TN).astype(BF)
    ug_ref[...] = dot(n_t, dgu[:, :, :, 1].reshape(rows, F), TN).astype(BF)

    wait(zbuf, r2_r)
    total = zbuf[0]
    for k in range(1, NZ):
        total = total + zbuf[k]
    picked = jnp.zeros((NE + 8, per), F32)
    for i in range(128 // per):
        picked = jnp.where(
            lax.rem(me_e, 128 // per) == i, total[:, i * per:(i + 1) * per], picked
        )
    rt_ref[...] = picked[:NE]
    gn_ref[...] = picked[NE:NE + 1]

    for kind, out in enumerate((act_ref, igr_ref)):
        for m in range(NM):
            wait(actb.at[kind, oc, m, c], ac_r.at[kind, m])
            for half in range(2):
                v = actb[kind, half, m, c].astype(F32)
                out[m, :, half * H:half * H + Q] = v[:8].astype(BF)
                out[m, :, half * H + Q:(half + 1) * H] = v[8:].astype(BF)

    for kind in range(2):
        wait(ebs.at[kind], e_s.at[kind])
        p, r = ((ps_f, rf), (ps_b, rb))[kind]
        sends = me_l < NP - 1 if kind == 0 else me_l > 0
        origin = me_l == NP - 1 - kind
        for m in range(NM):
            wait(actb.at[kind, 0, m, 0], ac_s.at[kind, m])
            for s in range(2):
                wait(xall.at[kind, m, s, 0], fw_s.at[kind, m, s])
                wait(p.at[m, s], pr_s.at[kind, m, s])
                wait(r.at[m, s, pl.ds(0, NZ - 1)], rs_s.at[kind, m, s])

                @pl.when(sends)
                def _():
                    wait(xall.at[kind, m, s, 0], ag_s.at[kind, m, s])

                @pl.when(origin)
                def _():
                    wait(xall.at[kind, m, s, 0], ag0_s.at[kind, m, s])

    wait(pmall.at[pl.ds(0, NE - 1)], m_s)
    for m in range(NM):
        for i, ref in enumerate((hid, nsl)):
            wait(ref.at[pl.ds(0, ND - 1), m], y_s.at[i, m])
        wait(gsl.at[pl.ds(0, ND - 1), m, 0], y_s.at[2, m])
        wait(gsl.at[pl.ds(0, ND - 1), m, 0], yp_s.at[m])
        for s in range(2):
            wait(dgu.at[0, m, s], yd_s.at[0, m, s])
            wait(dgu.at[0, m, s], yd_s.at[1, m, s])
            wait(dgu.at[0, m, s], yf_s.at[m, s])
    for j in range(ND // 2):
        @pl.when(c * (ND // 2) + j != me_y)
        def _():
            wait(ybuf.at[0], r1_s.at[j])

    @pl.when(mine)
    def _():
        wait(zbuf, r2_s)
        wait(zbuf.at[pl.ds(0, NZ - 1)], r2_s)


def local(embedded, out_grad, norm_gain, router_weight, gate_weight, up_weight, down_weight, routing):
    NM, _, D = embedded.shape
    F = gate_weight.shape[-1]
    NE, ND, NP = lax.axis_size("expert"), lax.axis_size("dp"), lax.axis_size("pipe")
    NZ, H, Q, R, DS = NE // 2, D // 2, D // 4, NE * 4, D // ND
    QX = Q + 128
    V = pl.BlockSpec(memory_space=pltpu.VMEM)
    A = pl.BlockSpec(memory_space=pl.ANY)

    def vm(*shape):
        return pltpu.VMEM(shape, BF)

    def vf(*shape):
        return pltpu.VMEM(shape, F32)

    sem = pltpu.SemaphoreType.DMA
    unit = sem((2, NM, 2))
    shape = jax.ShapeDtypeStruct
    per = DS // NE
    results = pl.pallas_call(
        functools.partial(kernel, (NM, D, F, NE, ND, NP)),
        name="moe_layers",
        in_specs=[V, V, V, V, V, A, A, A],
        out_specs=[V] * 7,
        out_shape=[
            shape((NM, 8, D), BF), shape((NM, 8, D), BF), shape((DS, F), BF), shape((DS, F), BF),
            shape((F, DS), BF), shape((NE, per), F32), shape((1, per), F32),
        ],
        scratch_shapes=[
            vm(D, F), vm(D, F), vm(F, D), vm(F, D), vm(F, D), vm(D, F),
            vm(2, NM, 16, Q), vm(2, 2, NM, 16, Q),
            vf(NE, NM, 8, 128),
            vm(2, NM, 2, 2, NZ * 16, Q), vm(NM, 2, R, D), vm(NM, 2, R, D),
            vf(NM, 2, R, F), vf(NM, 2, R, F), vm(NM, 2, R, F),
            vf(NM, 2, R, 128), vf(NM, 2, R, 128), vf(NM, 2, R, NE),
            vm(NM, 2, R, H), vm(NM, 2, R, H), vm(NM, 2, R, H + 128), vm(NM, 2, R, H + 128),
            vf(NM, 2, R, H), vf(R, H + 128), vm(NM, 2, NZ * 16, Q), vm(NM, 2, NZ * 16, QX),
            vm(NM, 2, NZ, 16, Q), vm(NM, 2, NZ, 16, QX), vm(2, 2, NM, 2, 16, Q),
            vm(ND, NM, 2, R, DS), vm(ND, NM, 2, R, DS), vm(ND, NM, 2, R, F), vm(ND, NM, 2, 2, R, F),
            vf(NE + 8, H), vf(NE + 8, H), vf(ND, NE + 8, DS), vf(NE + 8, DS), vf(NZ, NE + 8, 128),
            sem((3,)), sem((2,)), sem((2,)), sem, sem,
            unit, unit, unit, unit, unit, unit, unit, unit, unit, sem((2, NM)), sem((2, NM)),
            sem((3, NM)), sem((3, NM)), unit, unit, sem((NM, 2)), sem((NM, 2)), sem((NM,)), sem((NM,)), sem((NM,)),
            sem((ND // 2,)), sem, sem, sem,
        ],
        compiler_params=pltpu.CompilerParams(
            collective_id=0, has_side_effects=True, vmem_limit_bytes=58 * 2**20
        ),
    )(
        embedded, out_grad, routing[0], norm_gain, router_weight[0].T,
        gate_weight[0, 0], up_weight[0, 0], down_weight[0, 0],
    )
    act, igr, gg, ug, dg, rt, gn = pl.pallas_call(
        hand_over,
        name="hand_over",
        in_specs=[A] * 7,
        out_specs=[A] * 7,
        out_shape=[shape(v.shape, v.dtype) for v in results],
        scratch_shapes=[pltpu.VMEM(v.shape, v.dtype) for v in results] + [sem((2, 7))],
        compiler_params=pltpu.CompilerParams(vmem_limit_bytes=58 * 2**20),
    )(*results)
    return (
        act[None], igr[None], gg[None, None], ug[None, None], dg[None, None], rt.T[None], gn,
    )


def solution(mesh):
    return jax.shard_map(
        local,
        mesh=mesh,
        in_specs=(
            P(None, ("dp", "expert"), None),
            P(None, ("dp", "expert"), None),
            P("pipe", None),
            P("pipe", None, None),
            P("pipe", "expert", None, None),
            P("pipe", "expert", None, None),
            P("pipe", "expert", None, None),
            P("pipe", None, ("dp", "expert"), None),
        ),
        out_specs=(
            P("pipe", None, ("dp", "expert"), None),
            P("pipe", None, ("dp", "expert"), None),
            P("pipe", "expert", "dp", None),
            P("pipe", "expert", "dp", None),
            P("pipe", "expert", None, "dp"),
            P("pipe", ("dp", "expert"), None),
            P("pipe", ("dp", "expert")),
        ),
        check_vma=False,
    )
```

```python
import functools

import jax
import jax.numpy as jnp
from jax import lax
from jax.experimental import pallas as pl
from jax.experimental.pallas import tpu as pltpu
from jax.sharding import PartitionSpec as P

EPSILON = 1e-06
MESH = pl.DeviceIdType.MESH
BF = jnp.bfloat16
F32 = jnp.float32
NN = (((1,), (0,)), ((), ()))
NT = (((1,), (1,)), ((), ()))
TN = (((0,), (0,)), ((), ()))


def dot(a, b, dims):
    return lax.dot_general(a, b, dims, preferred_element_type=F32)


def col(value):
    return jnp.sum(value, axis=-1, keepdims=True)


def fold(value):
    half = value.shape[1] // 2
    return jnp.concatenate([value[:, :half], value[:, half:]], axis=0)


def twice(value):
    return jnp.concatenate([value, value], axis=0)


def hand_over(*refs):
    sems = refs[21]
    count = range(7)
    come = [pltpu.make_async_copy(refs[i], refs[14 + i], sems.at[0, i]) for i in count]
    go = [pltpu.make_async_copy(refs[14 + i], refs[7 + i], sems.at[1, i]) for i in count]
    for move in come:
        move.start()
    for i in count:
        come[i].wait()
        go[i].start()
    for move in go:
        move.wait()


def kernel(
    sizes,
    emb_ref, og_ref, ids_ref, gain_ref, rw_ref, gate_hbm, up_hbm, down_hbm,
    act_ref, igr_ref, gg_ref, ug_ref, dg_ref, rt_ref, gn_ref,
    wg, wu, wd, wgt, wut, wdt, ebs, src0, pmall, xall, nrm, gfull, gpre, upre, hidb, invs, wst, lgs,
    ps_f, pr_f, ps_b, pr_b, qo_f, qo_b, qf, qb, rf, rb, actb,
    nsl, gsl, hid, dgu, racc, rgs, ybuf, ysum, zbuf,
    w_sem, e_s, e_r, m_s, m_r, ag0_s, ag_s, ag_r, fw_s, fw_r, pr_s, pr_rs, rs_s, rs_r, ac_s, ac_r,
    y_s, y_r, yd_s, yd_r, yf_s, yf_r, yl_r, yp_s, yp_r, r1_s, r1_r, r2_s, r2_r,
):
    NM, D, F, NE, ND, NP = sizes
    NZ, H, Q, R, DS = NE // 2, D // 2, D // 4, NE * 4, D // ND
    QX = Q + 128
    me_y = lax.axis_index("dp")
    me_l = lax.axis_index("pipe")
    me_e = lax.axis_index("expert")
    z = me_e // 2
    c = me_e % 2
    oc = 1 - c
    partner = {"expert": me_e + 1 - 2 * c}
    own_rows = pl.ds(pl.multiple_of(z * 16, 16), 16)
    own_tokens = pl.ds(pl.multiple_of(z * 8, 8), 8)
    own_half = pl.ds(pl.multiple_of(c * H, H), H)
    other_half = pl.ds(pl.multiple_of(oc * H, H), H)
    last = (me_l + 1) // NP
    far_first = sorted(range(1, NZ), key=lambda k: (-min(k, NZ - k), k))
    y_up, y_down = (me_y + 1) % ND, (me_y + ND - 1) % ND

    def send(src, dst, ss, rs, dev):
        pltpu.make_async_remote_copy(
            src_ref=src, dst_ref=dst, send_sem=ss, recv_sem=rs, device_id=dev, device_id_type=MESH
        ).start()

    def copy(src, dst, sem):
        pltpu.make_async_copy(src, dst, sem).start()

    def wait(ref, sem):
        pltpu.make_async_copy(ref, ref, sem).wait()

    copy(gate_hbm, wg, w_sem.at[0])
    copy(up_hbm, wu, w_sem.at[1])
    copy(down_hbm, wd, w_sem.at[2])

    barrier = pltpu.get_barrier_semaphore()

    def hello(dev):
        pl.semaphore_signal(barrier, inc=1, device_id=dev, device_id_type=MESH)

    hello(partner)
    for k in range(1, NZ):
        for cc in range(2):
            hello({"expert": 2 * ((z + k) % NZ) + cc})
    for j in range(1, ND):
        hello({"dp": (me_y + j) % ND})
    for step in (1, NP - 1):
        for k in range(NZ):
            hello({"pipe": (me_l + step) % NP, "expert": 2 * ((z + k) % NZ) + c})

    mine0 = (c == 0).astype(F32)
    for kind, ref in enumerate((emb_ref, og_ref)):
        for m in range(NM):
            v = ref[m].astype(F32)
            low, high = v[:, :H], v[:, H:]
            src0[kind, c, m] = fold(low * mine0 + high * (1.0 - mine0)).astype(BF)
            ebs[kind, m] = fold(high * mine0 + low * (1.0 - mine0)).astype(BF)
    lanes8 = lax.broadcasted_iota(jnp.int32, (8, 128), 1)
    for m in range(NM):
        ids = ids_ref[m]
        table = jnp.zeros((8, 128), F32)
        for k in range(ids.shape[1]):
            table = table + (ids[:, k:k + 1] == lanes8).astype(F32)
        pmall[c * NZ + z, m] = table
    racc[...] = jnp.zeros(racc.shape, F32)

    pl.semaphore_wait(barrier, 1 + 2 * (NZ - 1) + (ND - 1) + 2 * NZ)

    for kind in range(2):
        send(ebs.at[kind], src0.at[kind, c], e_s.at[kind], e_r.at[kind], partner)
    my_table = pmall.at[c * NZ + z]
    send(my_table, my_table, m_s, m_r, partner)
    for k in range(1, NZ):
        for cc in range(2):
            send(my_table, my_table, m_s, m_r, {"expert": 2 * ((z + k) % NZ) + cc})

    def gather(kind, m, s, src, sems, section):
        for k in far_first + [0]:
            send(
                src, xall.at[kind, m, s, c, own_rows], sems.at[kind, m, s], ag_r.at[kind, m, s],
                {"pipe": section, "expert": 2 * ((z + k) % NZ) + c},
            )

    for kind in range(2):
        wait(src0.at[kind, oc], e_r.at[kind])

        @pl.when(me_l == NP - 1 - kind)
        def _():
            for m in range(NM):
                for s in range(2):
                    gather(kind, m, s, src0.at[kind, s, m], ag0_s, (NP - 1) * kind)

    wait(pmall.at[pl.ds(0, NE - 1)], m_r)
    wait(wg, w_sem.at[0])
    wait(wu, w_sem.at[1])
    wait(wd, w_sem.at[2])
    for j in range(D // 256):
        rows = slice(256 * j, 256 * j + 256)
        wgt[:, rows] = wg[rows, :].T
        wut[:, rows] = wu[rows, :].T
        wdt[rows, :] = wd[:, rows].T

    def arrive(kind, m, s):
        got = xall.at[kind, m, s, c]
        wait(got, ag_r.at[kind, m, s])
        send(got, got, fw_s.at[kind, m, s], fw_r.at[kind, m, s], partner)
        wait(xall.at[kind, m, s, oc], fw_r.at[kind, m, s])

    @pl.when(last == 1)
    def _():
        for m in range(NM):
            for s in range(2):
                arrive(1, m, s)

    def quarters(kind, m, s):
        out = []
        for half in range(2):
            v = xall[kind, m, s, half].astype(F32).reshape(NZ, 2, 8, Q)
            out += [v[:, 0].reshape(R, Q), v[:, 1].reshape(R, Q)]
        return out

    lane_e = lax.broadcasted_iota(jnp.int32, (R, NE), 1)
    lane_x = lax.broadcasted_iota(jnp.int32, (R, 128), 1)

    def forward_compute(m, s):
        xs = quarters(0, m, s)
        square = xs[0] * xs[0]
        for v in xs[1:]:
            square = square + v * v
        inv = lax.rsqrt(col(square) * (1.0 / D) + EPSILON)
        for i, v in enumerate(xs):
            nrm[m, s, :, i * Q:(i + 1) * Q] = (v * inv * gain_ref[0:1, i * Q:(i + 1) * Q]).astype(BF)
        normed = nrm[m, s]
        logits = dot(normed, rw_ref[...], NT)
        named = pmall[pl.ds(s * NZ, NZ), m].reshape(R, 128)[:, :NE]
        chosen = named * jax.nn.sigmoid(logits)
        w = col(jnp.where(lane_e == me_e, chosen, 0.0)) / col(chosen)
        invs[m, s] = jnp.broadcast_to(inv, (R, 128))
        wst[m, s] = jnp.broadcast_to(w, (R, 128))
        lgs[m, s] = logits
        a = dot(normed, wg[...], NN)
        b = dot(normed, wu[...], NN)
        gpre[m, s] = a
        upre[m, s] = b
        h = (a * jax.nn.sigmoid(a) * b).astype(BF)
        hidb[m, s] = h
        hid[me_y, m, s] = (h.astype(F32) * w).astype(BF)
        ps_f[m, s] = (dot(h, wd[:, other_half], NN) * w).astype(BF)
        send(ps_f.at[m, s], pr_f.at[m, s], pr_s.at[0, m, s], pr_rs.at[0, m, s], partner)
        qo_f[m, s] = dot(h, wd[:, own_half], NN) * w

    def scatter(kind, m, s, q, r):
        for k in far_first:
            zz = (z + k) % NZ
            send(
                q.at[m, s, pl.ds(pl.multiple_of(zz * 16, 16), 16)], r.at[m, s, z],
                rs_s.at[kind, m, s], rs_r.at[kind, m, s], {"expert": 2 * zz + c},
            )
        copy(q.at[m, s, own_rows], r.at[m, s, z], rs_r.at[kind, m, s])

    def part(ref, yy):
        return ref.at[:, pl.ds(pl.multiple_of(yy * DS, DS), DS)]

    def folded(v):
        width = v.shape[1] // 2
        low, high = v[:, :width].reshape(NZ, 1, 8, width), v[:, width:].reshape(NZ, 1, 8, width)
        return jnp.concatenate([low, high], axis=1).reshape(NZ * 16, width)

    def forward_scatter(m, s):
        wait(pr_f.at[m, s], pr_rs.at[0, m, s])
        qf[m, s] = folded(qo_f[m, s] + pr_f[m, s].astype(F32)).astype(BF)
        scatter(0, m, s, qf, rf)

    def forward_replicas(m, s):
        for j in range(1, ND):
            yy = (me_y + j) % ND
            mine = hid.at[me_y, m, s]
            send(mine, mine, y_s.at[0, m], y_r.at[0, m], {"dp": yy})
            send(part(nrm.at[m, s], yy), nsl.at[me_y, m, s], y_s.at[1, m], y_r.at[1, m], {"dp": yy})
        copy(part(nrm.at[m, s], me_y), nsl.at[me_y, m, s], y_r.at[1, m])

    def keep(kind, m, s):
        block = actb.at[kind, c, m, s]

        @pl.when(oc == s)
        def _():
            send(block, block, ac_s.at[kind, m], ac_r.at[kind, m], partner)

    def forward_result(m, s):
        wait(rf.at[m, s], rs_r.at[0, m, s])
        total = xall[0, m, s, c, own_rows].astype(F32)
        for k in range(NZ):
            total = total + rf[m, s, k].astype(F32)
        actb[0, c, m, s] = total.astype(BF)

        @pl.when(last == 0)
        def _():
            gather(0, m, s, actb.at[0, c, m, s], ag_s, me_l + 1)

        keep(0, m, s)

    def backward_compute(m, s):
        for i, v in enumerate(quarters(1, m, s)):
            gfull[m, s, :, i * Q:(i + 1) * Q] = v.astype(BF)
        dh = dot(gfull[m, s], wdt[...], NN)
        w = wst[m, s][:, :1]
        a = gpre[m, s]
        b = upre[m, s]
        dw = col(dh * hidb[m, s].astype(F32))
        dhw = dh * w
        sg = jax.nn.sigmoid(a)
        dgate = (dhw * b * sg * (1.0 + a * (1.0 - sg))).astype(BF)
        dupv = (dhw * (a * sg)).astype(BF)
        dgu[me_y, m, s, 0] = dgate
        dgu[me_y, m, s, 1] = dupv
        sv = col(dgate.astype(F32) * a + dupv.astype(F32) * b)
        dw_hi = dw.astype(BF).astype(F32)
        sv_hi = sv.astype(BF).astype(F32)
        ext = jnp.where(lane_x == me_e, dw_hi, 0.0)
        ext = jnp.where(lane_x == NE + me_e, dw - dw_hi, ext)
        ext = jnp.where(lane_x == 2 * NE + me_e, sv_hi, ext)
        ext = jnp.where(lane_x == 3 * NE + me_e, sv - sv_hi, ext)
        ps_b[m, s, :, :H] = (
            dot(dgate, wgt[:, other_half], NN) + dot(dupv, wut[:, other_half], NN)
        ).astype(BF)
        ps_b[m, s, :, H:] = ext.astype(BF)
        send(ps_b.at[m, s], pr_b.at[m, s], pr_s.at[1, m, s], pr_rs.at[1, m, s], partner)
        qo_b[:, :H] = dot(dgate, wgt[:, own_half], NN) + dot(dupv, wut[:, own_half], NN)
        qo_b[:, H:] = ext

    def backward_scatter(m, s):
        wait(pr_b.at[m, s], pr_rs.at[1, m, s])
        q = qo_b[...] + pr_b[m, s].astype(F32)
        qb[m, s, :, :Q] = folded(q[:, :H]).astype(BF)
        ext = q[:, H:].reshape(NZ, 1, 8, 128)
        qb[m, s, :, Q:] = (
            jnp.concatenate([ext, jnp.zeros_like(ext)], axis=1).reshape(NZ * 16, 128).astype(BF)
        )
        scatter(1, m, s, qb, rb)

    def backward_replicas(m, s):
        mine = dgu.at[me_y, m, s]
        send(mine, mine, yd_s.at[0, m, s], yd_r.at[0, m, s], {"dp": y_up})
        send(mine, mine, yd_s.at[1, m, s], yd_r.at[1, m, s], {"dp": y_down})
        copy(part(gfull.at[m, s], me_y), gsl.at[me_y, m, s], yl_r.at[m])

        @pl.when(s == c)
        def _():
            for j in range(1, ND):
                yy = (me_y + j) % ND
                send(
                    part(gfull.at[m, s], yy), gsl.at[me_y, m, s], y_s.at[2, m], y_r.at[2, m],
                    {"dp": yy},
                )

    def pass_on(m):
        for s, source, target in ((0, y_down, y_up), (1, y_up, y_down)):
            block = dgu.at[source, m, s]
            wait(block, yd_r.at[s, m, s])
            send(block, block, yf_s.at[m, s], yf_r.at[m, s], {"dp": target})
        wait(gsl.at[pl.ds(0, ND - 1), m, 0], y_r.at[2, m])
        for j in range(1, ND):
            block = gsl.at[(me_y + j) % ND, m, c]
            send(block, block, yp_s.at[m], yp_r.at[m], partner)

    def backward_result(m, s):
        wait(rb.at[m, s], rs_r.at[1, m, s])
        total = rb[m, s, 0].astype(F32)
        for k in range(1, NZ):
            total = total + rb[m, s, k].astype(F32)
        ext = total[:8, Q:]
        dw = ext[:, :NE] + ext[:, NE:2 * NE]
        sv = col(ext[:, 2 * NE:3 * NE] + ext[:, 3 * NE:4 * NE])
        logits = lgs[m, s, own_tokens]
        named = pmall[s * NZ + z, m][:, :NE]
        chosen = named * jax.nn.sigmoid(logits)
        prob_total = col(chosen)
        weights = chosen / prob_total
        dchosen = (dw - col(dw * weights)) / prob_total
        dlogits = dchosen * chosen * (1.0 - chosen)
        dl_hi = dlogits.astype(BF).astype(F32)
        dl = jnp.concatenate([dl_hi, dlogits - dl_hi], axis=0).astype(BF)
        term = dot(dl, rw_ref[:, own_half], NN)
        dnormed = total[:, :Q] + fold(term[:8] + term[8:])
        inv = twice(invs[m, s, own_tokens][:, :1])
        gain_row = gain_ref[0:1, own_half]
        gain = jnp.concatenate(
            [jnp.broadcast_to(gain_row[:, :Q], (8, Q)), jnp.broadcast_to(gain_row[:, Q:], (8, Q))],
            axis=0,
        )
        x = xall[0, m, s, c, own_rows].astype(F32)
        g = xall[1, m, s, c, own_rows].astype(F32)
        along = twice((sv + col(dlogits * logits)) * (1.0 / D))
        dinput = inv * (dnormed * gain - x * (inv * along))
        actb[1, c, m, s] = (g + dinput).astype(BF)

        @pl.when(me_l > 0)
        def _():
            gather(1, m, s, actb.at[1, c, m, s], ag_s, me_l - 1)

        keep(1, m, s)
        normed = x * inv * gain
        gained = dnormed * x * inv
        for i in range(2):
            rows = slice(8 * i, 8 * i + 8)
            cols = slice(Q * i, Q * i + Q)
            racc[0:NE, cols] = racc[0:NE, cols] + dot(dl, twice(normed[rows]).astype(BF), TN)
            racc[NE:NE + 8, cols] = racc[NE:NE + 8, cols] + gained[rows]

    units = 2 * NM

    def step(k, carry):
        u = k % units
        m, s = u // 2, u % 2
        before = (u + units - 1) % units
        bm, bs = before // 2, before % 2
        first = k < units
        is_last = last == 1
        forward = (first & (last == 0)) | ((k >= units) & is_last)
        backward = ((k >= units) & (last == 0)) | (first & is_last)

        @pl.when(first)
        def _():
            arrive(0, m, s)
            forward_compute(m, s)

        @pl.when(backward & (last == 0))
        def _():
            arrive(1, m, s)

        @pl.when(backward)
        def _():
            backward_compute(m, s)
            backward_replicas(m, s)

        @pl.when(forward)
        def _():
            forward_scatter(m, s)

        @pl.when(backward)
        def _():
            backward_scatter(m, s)

        @pl.when(forward & (u > 0))
        def _():
            forward_result(bm, bs)

        @pl.when(backward & (u > 0))
        def _():
            backward_result(bm, bs)

        @pl.when(forward)
        def _():
            forward_replicas(m, s)

        @pl.when(backward & (s == 1) & (m > 0))
        def _():
            pass_on(m - 1)

        @pl.when(forward & (u == units - 1))
        def _():
            forward_result(m, s)

        @pl.when(backward & (u == units - 1))
        def _():
            backward_result(m, s)

        return carry

    lax.fori_loop(0, 2 * units, step, 0)

    rgs[0:NE] = racc[0:NE]
    rgs[NE:NE + 8] = jnp.broadcast_to(
        jnp.sum(racc[NE:NE + 8], axis=0, keepdims=True), (8, H)
    )
    mine = c == me_y // (ND // 2)
    for j in range(ND // 2):
        yy = c * (ND // 2) + j
        src = rgs.at[:, pl.ds(j * DS, DS)]

        @pl.when(yy != me_y)
        def _():
            send(src, ybuf.at[me_y], r1_s.at[j], r1_r, {"dp": yy})

        @pl.when(yy == me_y)
        def _():
            copy(src, ybuf.at[me_y], r1_r)

    pass_on(NM - 1)
    per = DS // NE

    @pl.when(mine)
    def _():
        wait(ybuf, r1_r)
        total = ybuf[0]
        for j in range(1, ND):
            total = total + ybuf[j]
        ysum[...] = total
        for k in range(NZ):
            for cc in range(2):
                ee = 2 * ((z + k) % NZ) + (c + cc) % 2
                src = ysum.at[:, pl.ds(pl.multiple_of(ee * per // 128 * 128, 128), 128)]
                if k == 0 and cc == 0:
                    copy(src, zbuf.at[z], r2_r)
                else:
                    send(src, zbuf.at[z], r2_s, r2_r, {"expert": ee})

    far = (me_y + 2) % ND
    rows = ND * NM * 2 * R
    for m in range(NM):
        wait(hid.at[pl.ds(0, ND - 1), m], y_r.at[0, m])
        wait(nsl.at[:, m], y_r.at[1, m])
        wait(gsl.at[0, m], yl_r.at[m])
        wait(gsl.at[pl.ds(0, ND - 1), m, 0], yp_r.at[m])
    dg_ref[...] = dot(hid[...].reshape(rows, F), gsl[...].reshape(rows, DS), TN).astype(BF)

    for m in range(NM):
        for s in range(2):
            wait(dgu.at[y_down, m, s], yd_r.at[1 - s, m, s])
            wait(dgu.at[far, m, s], yf_r.at[m, s])
    n_t = nsl[...].reshape(rows, DS)
    gg_ref[...] = dot(n_t, dgu[:, :, :, 0].reshape(rows, F), TN).astype(BF)
    ug_ref[...] = dot(n_t, dgu[:, :, :, 1].reshape(rows, F), TN).astype(BF)

    wait(zbuf, r2_r)
    total = zbuf[0]
    for k in range(1, NZ):
        total = total + zbuf[k]
    picked = jnp.zeros((NE + 8, per), F32)
    for i in range(128 // per):
        picked = jnp.where(
            lax.rem(me_e, 128 // per) == i, total[:, i * per:(i + 1) * per], picked
        )
    rt_ref[...] = picked[:NE]
    gn_ref[...] = picked[NE:NE + 1]

    for kind, out in enumerate((act_ref, igr_ref)):
        for m in range(NM):
            wait(actb.at[kind, oc, m, c], ac_r.at[kind, m])
            for half in range(2):
                v = actb[kind, half, m, c].astype(F32)
                out[m, :, half * H:half * H + Q] = v[:8].astype(BF)
                out[m, :, half * H + Q:(half + 1) * H] = v[8:].astype(BF)

    for kind in range(2):
        wait(ebs.at[kind], e_s.at[kind])
        p, r = ((ps_f, rf), (ps_b, rb))[kind]
        sends = me_l < NP - 1 if kind == 0 else me_l > 0
        origin = me_l == NP - 1 - kind
        for m in range(NM):
            wait(actb.at[kind, 0, m, 0], ac_s.at[kind, m])
            for s in range(2):
                wait(xall.at[kind, m, s, 0], fw_s.at[kind, m, s])
                wait(p.at[m, s], pr_s.at[kind, m, s])
                wait(r.at[m, s, pl.ds(0, NZ - 1)], rs_s.at[kind, m, s])

                @pl.when(sends)
                def _():
                    wait(xall.at[kind, m, s, 0], ag_s.at[kind, m, s])

                @pl.when(origin)
                def _():
                    wait(xall.at[kind, m, s, 0], ag0_s.at[kind, m, s])

    wait(pmall.at[pl.ds(0, NE - 1)], m_s)
    for m in range(NM):
        for i, ref in enumerate((hid, nsl)):
            wait(ref.at[pl.ds(0, ND - 1), m], y_s.at[i, m])
        wait(gsl.at[pl.ds(0, ND - 1), m, 0], y_s.at[2, m])
        wait(gsl.at[pl.ds(0, ND - 1), m, 0], yp_s.at[m])
        for s in range(2):
            wait(dgu.at[0, m, s], yd_s.at[0, m, s])
            wait(dgu.at[0, m, s], yd_s.at[1, m, s])
            wait(dgu.at[0, m, s], yf_s.at[m, s])
    for j in range(ND // 2):
        @pl.when(c * (ND // 2) + j != me_y)
        def _():
            wait(ybuf.at[0], r1_s.at[j])

    @pl.when(mine)
    def _():
        wait(zbuf, r2_s)
        wait(zbuf.at[pl.ds(0, NZ - 1)], r2_s)


def local(embedded, out_grad, norm_gain, router_weight, gate_weight, up_weight, down_weight, routing):
    NM, _, D = embedded.shape
    F = gate_weight.shape[-1]
    NE, ND, NP = lax.axis_size("expert"), lax.axis_size("dp"), lax.axis_size("pipe")
    NZ, H, Q, R, DS = NE // 2, D // 2, D // 4, NE * 4, D // ND
    QX = Q + 128
    V = pl.BlockSpec(memory_space=pltpu.VMEM)
    A = pl.BlockSpec(memory_space=pl.ANY)

    def vm(*shape):
        return pltpu.VMEM(shape, BF)

    def vf(*shape):
        return pltpu.VMEM(shape, F32)

    sem = pltpu.SemaphoreType.DMA
    unit = sem((2, NM, 2))
    shape = jax.ShapeDtypeStruct
    per = DS // NE
    results = pl.pallas_call(
        functools.partial(kernel, (NM, D, F, NE, ND, NP)),
        name="moe_layers",
        in_specs=[V, V, V, V, V, A, A, A],
        out_specs=[V] * 7,
        out_shape=[
            shape((NM, 8, D), BF), shape((NM, 8, D), BF), shape((DS, F), BF), shape((DS, F), BF),
            shape((F, DS), BF), shape((NE, per), F32), shape((1, per), F32),
        ],
        scratch_shapes=[
            vm(D, F), vm(D, F), vm(F, D), vm(F, D), vm(F, D), vm(D, F),
            vm(2, NM, 16, Q), vm(2, 2, NM, 16, Q),
            vf(NE, NM, 8, 128),
            vm(2, NM, 2, 2, NZ * 16, Q), vm(NM, 2, R, D), vm(NM, 2, R, D),
            vf(NM, 2, R, F), vf(NM, 2, R, F), vm(NM, 2, R, F),
            vf(NM, 2, R, 128), vf(NM, 2, R, 128), vf(NM, 2, R, NE),
            vm(NM, 2, R, H), vm(NM, 2, R, H), vm(NM, 2, R, H + 128), vm(NM, 2, R, H + 128),
            vf(NM, 2, R, H), vf(R, H + 128), vm(NM, 2, NZ * 16, Q), vm(NM, 2, NZ * 16, QX),
            vm(NM, 2, NZ, 16, Q), vm(NM, 2, NZ, 16, QX), vm(2, 2, NM, 2, 16, Q),
            vm(ND, NM, 2, R, DS), vm(ND, NM, 2, R, DS), vm(ND, NM, 2, R, F), vm(ND, NM, 2, 2, R, F),
            vf(NE + 8, H), vf(NE + 8, H), vf(ND, NE + 8, DS), vf(NE + 8, DS), vf(NZ, NE + 8, 128),
            sem((3,)), sem((2,)), sem((2,)), sem, sem,
            unit, unit, unit, unit, unit, unit, unit, unit, unit, sem((2, NM)), sem((2, NM)),
            sem((3, NM)), sem((3, NM)), unit, unit, sem((NM, 2)), sem((NM, 2)), sem((NM,)), sem((NM,)), sem((NM,)),
            sem((ND // 2,)), sem, sem, sem,
        ],
        compiler_params=pltpu.CompilerParams(
            collective_id=0, has_side_effects=True, vmem_limit_bytes=58 * 2**20
        ),
    )(
        embedded, out_grad, routing[0], norm_gain, router_weight[0].T,
        gate_weight[0, 0], up_weight[0, 0], down_weight[0, 0],
    )
    act, igr, gg, ug, dg, rt, gn = pl.pallas_call(
        hand_over,
        name="hand_over",
        in_specs=[A] * 7,
        out_specs=[A] * 7,
        out_shape=[shape(v.shape, v.dtype) for v in results],
        scratch_shapes=[pltpu.VMEM(v.shape, v.dtype) for v in results] + [sem((2, 7))],
        compiler_params=pltpu.CompilerParams(vmem_limit_bytes=58 * 2**20),
    )(*results)
    return (
        act[None], igr[None], gg[None, None], ug[None, None], dg[None, None], rt.T[None], gn,
    )


def solution(mesh):
    return jax.shard_map(
        local,
        mesh=mesh,
        in_specs=(
            P(None, ("dp", "expert"), None),
            P(None, ("dp", "expert"), None),
            P("pipe", None),
            P("pipe", None, None),
            P("pipe", "expert", None, None),
            P("pipe", "expert", None, None),
            P("pipe", "expert", None, None),
            P("pipe", None, ("dp", "expert"), None),
        ),
        out_specs=(
            P("pipe", None, ("dp", "expert"), None),
            P("pipe", None, ("dp", "expert"), None),
            P("pipe", "expert", "dp", None),
            P("pipe", "expert", "dp", None),
            P("pipe", "expert", None, "dp"),
            P("pipe", ("dp", "expert"), None),
            P("pipe", ("dp", "expert")),
        ),
        check_vma=False,
    )
```
